32 devices in a mesh: lon: 4 (over y, x), lat: 8 (over z, core).
Axes of the slice: x: 2, y: 2, z: 4, core: 2. Of those that a mesh axis runs over, the one named last changes fastest.
Arguments:
- adjoint_in: float32 [5, 192, 192, 128], P(None, 'lon', 'lat'), may hold values from -6 to 6
- departures: float32 [4, 8, 1024, 128], P('lon', 'lat'), may hold values from -6 to 6
- obs_band: int32 [4, 8, 1024, 1], P('lon', 'lat'), may hold values from 0 to 7; in each aligned block of 1024 rows (0 to 1023, 1024 to 2047, ..., all dimensions but the last counted through in order) at most 384 rows name the same one
- obs_station: int32 [4, 8, 1024], P('lon', 'lat'), may hold values from 0 to 511
- obs_var: int32 [4, 8, 1024], P('lon', 'lat'), may hold values from 0 to 4
- counts: int32 [4, 8], P('lon', 'lat'), may hold values from 512 to 1024, as said below
- station_cell: int32 [4, 8, 512], P('lon', 'lat'), may hold values from 0 to 1151
- coefficients: float32 [3, 192, 192, 128], P(None, 'lon', 'lat'), as said below
Outputs:
- adjoint_out: float32 [5, 192, 192, 128], P(None, 'lon', 'lat')
The draws below stay inside these ranges and needn't reach their ends.
Inputs may be any that keep to these rules, and one draw needn't show every extreme that they name: `obs_band`: among the 1024 blocks of one device at most 384 name the same band, and on some device exactly 384 do. `counts`: some device has exactly 1024 live blocks. `coefficients`: the diffusivity lies between 0.03 and 0.12.
All inputs are finite; a program needn't handle non-finite values.
Results may differ from the reference program's by a relative error of at most 0.00013.
Values sent between devices are 32-bit elements; how exact they have to be, the bound alone decides.
No kernel may reach another device: no remote copies, remote signals or barrier semaphores. Data moves between devices by JAX's collectives and lax.ppermute only.
A program may use at most 384 MiB of HBM per device.

```python
import math
import jax
import jax.numpy as jnp
import numpy as np
from jax import lax

VARS = 5
LEV = 128
LON_DEV = 48
LAT_DEV = 24
OBS_DEV = 1024
STATIONS = 512
LON_TILES = 4
LAT_BANDS = 8
NLON = 192
NLAT = 192
CAP = 384
N_LON = 4


def draw_counts(key, part):
    key = jax.random.fold_in(key, 5)
    first_key, second_key = jax.random.split(key)
    total = LON_TILES * LAT_BANDS
    values = jax.random.randint(first_key, (total,), OBS_DEV // 2, OBS_DEV + 1)
    chosen = jax.random.randint(second_key, (), 0, total)
    values = values.at[chosen].set(OBS_DEV)
    return values.reshape(LON_TILES, LAT_BANDS).astype(jnp.int32)


def draw_coefficients(key, part):
    key = jax.random.fold_in(key, 11)
    wind_key, kappa_key = jax.random.split(key)
    winds = jnp.clip(jax.random.normal(wind_key, (2, NLON, NLAT, LEV), jnp.float32), -4.0, 4.0)
    kappa = jnp.exp(jax.random.uniform(kappa_key, (1, NLON, NLAT, LEV), jnp.float32, jnp.log(0.03), jnp.log(0.12)))
    return jnp.concatenate([winds, kappa], 0).astype(jnp.float32)


def touch_ends(values, stream_key, smallest, top_value):
    longest = values.shape.index(max(values.shape))
    spots = []
    for shift in (0, 1):
        where = [jax.random.randint(jax.random.fold_in(stream_key, axis), (), 0, length) for axis, length in enumerate(values.shape)]
        where[longest] = (where[longest] + shift) % values.shape[longest]
        spots.append(tuple(where))
    return values.at[spots[0]].set(smallest).at[spots[1]].set(top_value)


def block_levels(stream_key, dims, cuts, low, top_value):
    def one(dim, blocks):
        draws = jax.random.uniform(jax.random.fold_in(jax.random.fold_in(stream_key, 6), dim), (blocks,), jnp.float32, low / len(cuts), top_value / len(cuts))
        return jnp.repeat(jnp.exp(draws), dims[dim] // blocks).reshape((-1,) + (1,) * (len(dims) - dim - 1))

    loudness = one(*cuts[0])
    for cut in cuts[1:]:
        loudness = loudness * one(*cut)
    return loudness


def shared_out(stream_key, own, number, rows, count, top, reach, skew):
    sequence = jax.random.permutation(stream_key, count)
    heavy_load, usual = load_shares(count, rows * top, reach, skew, True), load_shares(count, rows * top, reach, skew, False)
    places = jnp.arange(count)

    def named(tallies, offset_by):
        used = int((tallies > 0).sum())
        fixed = max(1, used // 4)
        moved = fixed + (places - fixed + offset_by * (used - fixed)) % max(1, count - fixed)
        return jnp.zeros((count,), jnp.int32).at[sequence[jnp.where(places < fixed, places, moved)]].set(jnp.asarray(tallies, jnp.int32))

    tallies = jnp.where(number % 4 == 0, named(heavy_load, number // 4), named(usual, number - number // 4 - 1))
    mixed = jax.random.permutation(jax.random.fold_in(own, 3), count)
    giver, receiver = mixed[0:count // 2 * 2:2], mixed[1:count // 2 * 2:2]
    margin = jnp.minimum(tallies[giver] - 1, reach - tallies[receiver]) // 2
    margin = jnp.where((giver == sequence[0]) | (receiver == sequence[0]) | (tallies[receiver] == 0), 0, jnp.maximum(margin, 0))
    moved = jax.random.randint(jax.random.fold_in(own, 4), (count // 2,), 0, 1 << 20) % (margin + 1)
    tallies = tallies.at[giver].add(-moved).at[receiver].add(moved)
    labels = jnp.searchsorted(jnp.cumsum(tallies), jnp.arange(rows * top), side="right").astype(jnp.int32)
    grid = labels.reshape(top, rows).T
    grid = grid[jax.random.permutation(jax.random.fold_in(own, 1), rows)]
    offset_by = jax.random.randint(jax.random.fold_in(own, 2), (rows, 1), 0, top)
    return jnp.take_along_axis(grid, (jnp.arange(top)[None, :] + offset_by) % top, axis=1)


def load_shares(number_of, total, bound, lean, full):
    portions = [(1 << 20) // math.isqrt(rank ** lean) + 1 for rank in range(1, number_of + 1)]
    largest = bound if full else min(bound, max(-(-total // number_of), total * portions[0] // sum(portions)))
    least = 1 if total - largest >= number_of - 1 else 0
    given, spare = [largest] + [least] * (number_of - 1), total - largest - least * (number_of - 1)
    while spare > 0:
        free = [i for i in range(1, number_of) if given[i] < largest] or [i for i in range(1, number_of) if given[i] < bound]
        whole, remaining = sum([portions[i] for i in free]), spare
        for i in free:
            more = min(bound - given[i], max(1, remaining * portions[i] // whole), spare)
            given[i] = given[i] + more
            spare = spare - more
    return np.array(given)


def normal_values(stream_key, shape, width, most, cuts=(), held_as=jnp.bfloat16):
    drawn = jax.random.normal(stream_key, shape, jnp.float32) * width
    if len(cuts) > 0:
        drawn = block_levels(stream_key, shape, cuts, -0.22, 0.18) * drawn
    return jnp.clip(drawn, min=-most, max=most).astype(held_as)


def setup_inputs(seed: int = 0) -> dict:
    key_list = jax.random.split(jax.random.key(seed), 9)
    adjoint_in = normal_values(key_list[0], (VARS, NLON, NLAT, LEV), 1.0, 6.0, ((1, 4), (2, 8)), jnp.float32)
    departures = normal_values(key_list[1], (LON_TILES, LAT_BANDS, OBS_DEV, LEV), 1.0, 6.0, ((0, 4), (1, 8)), jnp.float32)
    obs_band_keys = jax.random.split(jax.random.fold_in(key_list[2], 1), LON_TILES * LAT_BANDS * OBS_DEV // OBS_DEV)
    obs_band_turns = jax.random.permutation(jax.random.fold_in(key_list[2], 3), LON_TILES * LAT_BANDS * OBS_DEV // OBS_DEV)
    obs_band = jax.vmap(lambda own, number: shared_out(jax.random.fold_in(key_list[2], 2), own, number, OBS_DEV, LAT_BANDS, 1, CAP, 2))(obs_band_keys, obs_band_turns).reshape((LON_TILES, LAT_BANDS, OBS_DEV, 1))
    obs_station = touch_ends(jax.random.randint(key_list[3], (LON_TILES, LAT_BANDS, OBS_DEV), 0, STATIONS), jax.random.fold_in(key_list[3], 1), 0, STATIONS - 1).astype(jnp.int32)
    obs_var = touch_ends(jax.random.randint(key_list[4], (LON_TILES, LAT_BANDS, OBS_DEV), 0, VARS), jax.random.fold_in(key_list[4], 1), 0, VARS - 1).astype(jnp.int32)
    counts = draw_counts(jax.random.fold_in(key_list[8], 71), 0)
    station_cell = touch_ends(jax.random.randint(key_list[6], (LON_TILES, LAT_BANDS, STATIONS), 0, LON_DEV * LAT_DEV), jax.random.fold_in(key_list[6], 1), 0, (LON_DEV * LAT_DEV) - 1).astype(jnp.int32)
    coefficients = draw_coefficients(jax.random.fold_in(key_list[8], 71), 0)
    return {"adjoint_in": adjoint_in, "departures": departures, "obs_band": obs_band, "obs_station": obs_station, "obs_var": obs_var, "counts": counts, "station_cell": station_cell, "coefficients": coefficients}


ADVECT_SCALE = 0.2


def advance(padded, coeffs):
    centre = padded[:, 1:-1, 1:-1]
    east_side = padded[:, 2:, 1:-1]
    west_side = padded[:, :-2, 1:-1]
    north_side = padded[:, 1:-1, 2:]
    south_side = padded[:, 1:-1, :-2]
    wind_east = coeffs[0, 1:-1, 1:-1]
    wind_west = coeffs[0, :-2, 1:-1]
    wind_north = coeffs[1, 1:-1, 1:-1]
    wind_south = coeffs[1, 1:-1, :-2]
    kappa_all = coeffs[2]
    kappa_centre = kappa_all[1:-1, 1:-1]
    kappa_east = 0.5 * (kappa_centre + kappa_all[2:, 1:-1])
    kappa_west = 0.5 * (kappa_centre + kappa_all[:-2, 1:-1])
    kappa_north = 0.5 * (kappa_centre + kappa_all[1:-1, 2:])
    kappa_south = 0.5 * (kappa_centre + kappa_all[1:-1, :-2])
    level_zero = jnp.zeros_like(kappa_centre[..., :1])
    kappa_up = jnp.concatenate([0.5 * (kappa_centre[..., :-1] + kappa_centre[..., 1:]), level_zero], -1)
    kappa_down = jnp.concatenate([level_zero, kappa_up[..., :-1]], -1)
    centre_zero = jnp.zeros_like(centre[..., :1])
    above = jnp.concatenate([centre[..., 1:], centre_zero], -1)
    below = jnp.concatenate([centre_zero, centre[..., :-1]], -1)
    transport = wind_east * (east_side - centre) + wind_west * (centre - west_side)
    transport = transport + wind_north * (north_side - centre) + wind_south * (centre - south_side)
    mixing = kappa_east * (east_side - centre) - kappa_west * (centre - west_side)
    mixing = mixing + kappa_north * (north_side - centre) - kappa_south * (centre - south_side)
    mixing = mixing + kappa_up * (above - centre) - kappa_down * (centre - below)
    return centre + ADVECT_SCALE * transport + mixing


def extend(values):
    widened = jnp.pad(values, ((0, 0), (1, 1), (0, 0), (0, 0)), mode="wrap")
    return jnp.pad(widened, ((0, 0), (0, 0), (1, 1), (0, 0)))


def reference(adjoint_in, departures, obs_band, obs_station, obs_var, counts, station_cell, coefficients):
    tiles = jnp.arange(N_LON, dtype=jnp.int32)[:, None, None]
    bands = obs_band[..., 0]
    column = station_cell[tiles, bands, obs_station]
    glon = tiles * LON_DEV + column // LAT_DEV
    glat = bands * LAT_DEV + column % LAT_DEV
    target = obs_var * (NLON * NLAT) + glon * NLAT + glat
    live = (jnp.arange(OBS_DEV, dtype=jnp.int32)[None, None, :] < counts[:, :, None]).astype(departures.dtype)
    amounts = departures * live[..., None]
    flat_state = adjoint_in.reshape(VARS * NLON * NLAT, LEV)
    flat_state = flat_state.at[target.reshape(-1)].add(amounts.reshape(-1, LEV))
    forced = flat_state.reshape(VARS, NLON, NLAT, LEV)
    coeff_ext = extend(coefficients)

    def evolve(variable):
        current = variable[None]
        current = advance(extend(current), coeff_ext)
        current = advance(extend(current), coeff_ext)
        return current[0]

    return lax.map(evolve, forced)
```

```python
import functools

import jax
import jax.numpy as jnp
from jax import lax
from jax.experimental import pallas as pl
from jax.experimental.pallas import tpu as pltpu
from jax.sharding import PartitionSpec as P

ADVECT_SCALE = 0.2
LANES = 128
STRIDE = 1024
HEADER = 8
VMEM_LIMIT = 40 * 1024 * 1024
V = pltpu.VMEM


def in_vmem(array):
    return pltpu.with_memory_space_constraint(array, V)


def in_hbm(array):
    return pltpu.with_memory_space_constraint(array, pltpu.HBM)


def params():
    return pltpu.CompilerParams(vmem_limit_bytes=VMEM_LIMIT)


def start_all(copies):
    for copy in copies:
        copy.start()


def wait_all(copies):
    for copy in copies:
        copy.wait()


def run(copies):
    start_all(copies)
    wait_all(copies)


def pack_kernel(
    n, cap, stations, count_ref, band_ref, station_ref, var_ref, dep_ref, coef_ref, *rest
):
    half = n // 2
    own, swap = rest[:2]
    through = rest[2 : half + 1]
    south, north = rest[half + 1 : half + 3]
    (dep, band, station, var, low, high, buf, pos_v, pos_s, sem) = rest[half + 3 :]
    me = lax.axis_index("lat")
    rows, lanes = band.shape
    lat_cells = coef_ref.shape[2]
    loads = [
        pltpu.make_async_copy(src, dst, sem.at[k])
        for k, (src, dst) in enumerate(
            (
                (band_ref, band),
                (station_ref, station),
                (var_ref, var),
                (dep_ref, dep),
                (coef_ref.at[:, :, pl.ds(0, 8)], low),
                (coef_ref.at[:, :, pl.ds(lat_cells - 8, 8)], high),
            )
        )
    ]
    start_all(loads)
    wait_all(loads[:3])
    count = count_ref[0, 0]
    slot = (
        lax.broadcasted_iota(jnp.int32, (rows, lanes), 0) * lanes
        + lax.broadcasted_iota(jnp.int32, (rows, lanes), 1)
    )
    far = (band[...] >> 1) - (me >> 1)
    far = jnp.where(far < 0, far + half, far)
    group = jnp.where((band[...] & 1) == (me & 1), far, far + half)
    group = jnp.where(slot < count, group, n)
    masks = jnp.concatenate([(group == s).astype(jnp.float32) for s in range(n)], axis=0)
    before = lax.broadcasted_iota(jnp.int32, (lanes, lanes), 0) < lax.broadcasted_iota(
        jnp.int32, (lanes, lanes), 1
    )
    prefix = jnp.dot(masks, before.astype(jnp.float32), preferred_element_type=jnp.float32)
    totals = jnp.dot(
        masks, jnp.ones((lanes, lanes), jnp.float32), preferred_element_type=jnp.float32
    )
    a = lax.broadcasted_iota(jnp.int32, (rows * n, rows * n), 0)
    b = lax.broadcasted_iota(jnp.int32, (rows * n, rows * n), 1)
    earlier = ((a // rows == b // rows) & (b < a)).astype(jnp.float32)
    offset = jnp.dot(earlier, totals, preferred_element_type=jnp.float32)
    ranks = (prefix + offset).astype(jnp.int32)
    rank = jnp.zeros((rows, lanes), jnp.int32)
    for s in range(n):
        rank = jnp.where(group == s, ranks[s * rows : (s + 1) * rows], rank)
    pos_v[...] = group * STRIDE + rank
    place_map = pltpu.make_async_copy(pos_v, pos_s, sem.at[0])
    place_map.start()
    code = var[...] * stations + station[...]
    upper = (code >> 6).astype(jnp.float32)
    lower = (code & 63).astype(jnp.float32)
    width = -(-cap // lanes) * lanes
    which = lax.broadcasted_iota(jnp.int32, (n, lanes), 0)
    order = lax.broadcasted_iota(jnp.int32, (width, lanes), 0)
    codes = jnp.zeros((2 * n, width), jnp.float32)
    for k in range(rows):
        mine = which == group[k : k + 1]
        parts = jnp.concatenate(
            [jnp.where(mine, upper[k : k + 1], 0.0), jnp.where(mine, lower[k : k + 1], 0.0)], 0
        )
        codes += lax.dot_general(
            parts,
            (order == rank[k : k + 1]).astype(jnp.float32),
            (((1,), (1,)), ((), ())),
            preferred_element_type=jnp.float32,
        )
    codes = codes[:n] * 64.0 + codes[n:]
    counts = offset + totals
    size = cap + HEADER

    def target(s):
        if s == 0:
            return own, 0
        if s < half:
            return through[s - 1], 0
        return swap, (s - half) * size

    for s in range(n):
        to, at = target(s)
        for j in range(width // lanes):
            to[pl.ds(at + cap + j, 1), :] = codes[s : s + 1, j * lanes : (j + 1) * lanes]
        to[pl.ds(at + cap + HEADER - 1, 1), :] = counts[(s + 1) * rows - 1 : (s + 1) * rows]
    wait_all(loads[3:])
    fields, lons = low.shape[:2]

    def strip(i, carry):
        for f in range(fields):
            north[pl.ds((f * lons + i) * 2, 2), :] = high[f, i, 6:8]
            south[pl.ds((f * lons + i) * 2, 2), :] = low[f, i, 0:2]
        return carry

    lax.fori_loop(0, lons, strip, 0)
    place_map.wait()

    def place(g, carry):
        base = pl.multiple_of(g * 16, 16)
        row, col = base >> 7, base & 127
        for k in range(16):
            buf[pl.ds(pos_s[row, col + k], 1), :] = dep[pl.ds(base + k, 1), :]
        return carry

    lax.fori_loop(0, (count + 15) >> 4, place, 0)
    for s in range(n):
        to, at = target(s)
        to[pl.ds(at, cap), :] = buf[pl.ds(s * STRIDE, cap), :]


def pack(n, cap, stations, count, band, station, var, dep, coef):
    rows = dep.shape[0] // LANES
    fields, lons = coef.shape[:2]
    size, half = cap + HEADER, n // 2
    strip = (fields * lons * 2, LANES)
    shapes = [(size, LANES), (half * size, LANES)]
    shapes += [(2 * size, LANES)] * (half - 1) + [strip, strip]
    hbm = pl.BlockSpec(memory_space=pltpu.HBM)
    vm = pl.BlockSpec(memory_space=V)
    return pl.pallas_call(
        functools.partial(pack_kernel, n, cap, stations),
        out_shape=tuple(V(shape, jnp.float32) for shape in shapes),
        in_specs=[pl.BlockSpec(memory_space=pltpu.SMEM)] + [hbm] * 5,
        out_specs=(vm,) * len(shapes),
        scratch_shapes=[
            V(dep.shape, jnp.float32),
            V((rows, LANES), jnp.int32),
            V((rows, LANES), jnp.int32),
            V((rows, LANES), jnp.int32),
            V((fields, lons, 8, LANES), jnp.float32),
            V((fields, lons, 8, LANES), jnp.float32),
            V((n * STRIDE + HEADER + STRIDE, LANES), jnp.float32),
            V((rows, LANES), jnp.int32),
            pltpu.SMEM((rows, LANES), jnp.int32),
            pltpu.SemaphoreType.DMA((6,)),
        ],
        compiler_params=params(),
        name="pack",
    )(count, *(in_hbm(array) for array in (band, station, var, dep, coef)))


def relay_kernel(k, size, swapped, *rest):
    for j, to in enumerate(rest[k:]):
        to[pl.ds(size, size), :] = swapped[pl.ds((j + 1) * size, size), :]


def relay(swapped, through, size):
    k = len(through)
    vm = pl.BlockSpec(memory_space=V)
    return pl.pallas_call(
        functools.partial(relay_kernel, k, size),
        out_shape=tuple(V(array.shape, jnp.float32) for array in through),
        in_specs=[vm] * (k + 1),
        out_specs=(vm,) * k,
        input_output_aliases={j + 1: j for j in range(k)},
        compiler_params=params(),
        name="relay",
    )(in_vmem(swapped), *(in_vmem(array) for array in through))


def open_header(packet, base, cap, view, header, sem):
    view[...] = packet[pl.ds(base + cap, HEADER), :].astype(jnp.int32)
    copy = pltpu.make_async_copy(view, header, sem)
    copy.start()
    return copy


def scatter_packet(table_ref, packet, start, header, state):
    unroll = 8
    count = header[HEADER - 1, 0]

    def some(g, carry):
        base = g * unroll
        major, minor = base >> 7, base & 127
        rows = [table_ref[0, header[major, minor + k]] for k in range(unroll)]
        for k in range(unroll):
            state[pl.ds(rows[k], 1), :] += packet[pl.ds(start + base + k, 1), :]
        return carry

    def one(j, carry):
        row = table_ref[0, header[j >> 7, j & 127]]
        state[pl.ds(row, 1), :] += packet[pl.ds(start + j, 1), :]
        return carry

    whole = count >> 3
    lax.fori_loop(0, whole, some, 0)
    lax.fori_loop(whole * unroll, count, one, 0)


def first_kernel(
    lons, lats, cap, table_ref, adjoint_ref, own_ref, swap_ref, state, full, *rest
):
    views, headers, sem = rest[:2], rest[2:4], rest[4]
    span = lats + 4
    ring = (lons + 4) * span
    nv = state.shape[0] // ring
    load = pltpu.make_async_copy(adjoint_ref, full, sem.at[0])
    load.start()
    packets = (own_ref, swap_ref)
    opened = [
        open_header(packets[j], 0, cap, views[j], headers[j], sem.at[j + 1]) for j in range(2)
    ]
    load.wait()

    def fill(i, carry):
        for v in range(nv):
            to = v * ring + (i + 2) * span + 2
            at = (v * lons + i) * lats
            for r in range(0, lats, 8):
                state[pl.ds(to + r, 8), :] = full[pl.ds(pl.multiple_of(at + r, 8), 8), :]
        return carry

    lax.fori_loop(0, lons, fill, 0)
    wait_all(opened)
    for j in range(2):
        scatter_packet(table_ref, packets[j], 0, headers[j], state)


def scatter_first(table, adjoint, own, swapped, cap, shape):
    nv, lons, lats = shape
    hbm = pl.BlockSpec(memory_space=pltpu.HBM)
    ring = (lons + 4) * (lats + 4)
    return pl.pallas_call(
        functools.partial(first_kernel, lons, lats, cap),
        out_shape=V((nv * ring, LANES), jnp.float32),
        in_specs=[pl.BlockSpec(memory_space=pltpu.SMEM), hbm] + [pl.BlockSpec(memory_space=V)] * 2,
        out_specs=pl.BlockSpec(memory_space=V),
        scratch_shapes=[
            V(adjoint.shape, jnp.float32),
            V((HEADER, LANES), jnp.int32),
            V((HEADER, LANES), jnp.int32),
            pltpu.SMEM((HEADER, LANES), jnp.int32),
            pltpu.SMEM((HEADER, LANES), jnp.int32),
            pltpu.SemaphoreType.DMA((3,)),
        ],
        compiler_params=params(),
        name="scatter_own",
    )(table, in_hbm(adjoint), in_vmem(own), in_vmem(swapped))


def more_kernel(k, lons, lats, cap, last, table_ref, *rest):
    packets = [(rest[j], base) for j in range(k) for base in (0, cap + HEADER)]
    m = len(packets)
    rest = rest[len(rest) - (3 if last else 1) - 2 * m - 1 :]
    outs, rest = rest[: 3 if last else 1], rest[3 if last else 1 :]
    views, headers, sem = rest[:m], rest[m : 2 * m], rest[2 * m]
    state = outs[0]
    opened = [
        open_header(*packets[j], cap, views[j], headers[j], sem.at[j]) for j in range(m)
    ]
    wait_all(opened)
    for j in range(m):
        scatter_packet(table_ref, *packets[j], headers[j], state)
    if not last:
        return
    south, north = outs[1:]
    span = lats + 4
    ring = (lons + 4) * span
    nv = state.shape[0] // ring

    def strip(i, carry):
        for v in range(nv):
            at = v * ring + (i + 2) * span
            to = (v * lons + i) * 2
            south[pl.ds(to, 2), :] = state[pl.ds(at + 2, 2), :]
            north[pl.ds(to, 2), :] = state[pl.ds(at + lats, 2), :]
        return carry

    lax.fori_loop(0, lons, strip, 0)


def scatter_more(table, state, packets, cap, shape, last, after=()):
    nv, lons, lats = shape
    k = len(packets)
    vm = pl.BlockSpec(memory_space=V)
    out = V(state.shape, jnp.float32)
    strip = V((nv * lons * 2, LANES), jnp.float32)
    return pl.pallas_call(
        functools.partial(more_kernel, k, lons, lats, cap, last),
        out_shape=(out, strip, strip) if last else out,
        in_specs=[pl.BlockSpec(memory_space=pltpu.SMEM)] + [vm] * (k + 1 + len(after)),
        out_specs=(vm, vm, vm) if last else vm,
        input_output_aliases={k + 1: 0},
        scratch_shapes=[V((HEADER, LANES), jnp.int32)] * (2 * k)
        + [pltpu.SMEM((HEADER, LANES), jnp.int32)] * (2 * k)
        + [pltpu.SemaphoreType.DMA((2 * k,))],
        compiler_params=params(),
        name="scatter_last" if last else "scatter_more",
    )(
        table,
        *(in_vmem(packet) for packet in packets),
        in_vmem(state),
        *(in_vmem(array) for array in after),
    )


def widen_kernel(coef_ref, south_ref, north_ref, ring_out, west, east, own, sem):
    fields, lons, lats, _ = coef_ref.shape
    span = lats + 4
    ring = (lons + 4) * span
    me = lax.axis_index("lat")
    has_south = (me > 0).astype(jnp.float32)
    has_north = (me < lax.axis_size("lat") - 1).astype(jnp.float32)
    run([pltpu.make_async_copy(coef_ref, own, sem)])

    def fill(i, carry):
        for f in range(fields):
            to = f * ring + (i + 2) * span
            at = (f * lons + i) * 2
            for r in range(0, lats, 8):
                ring_out[pl.ds(to + 2 + r, 8), :] = own[f, i, r : r + 8]
            ring_out[pl.ds(to, 2), :] = south_ref[pl.ds(at, 2), :] * has_south
            ring_out[pl.ds(to + lats + 2, 2), :] = north_ref[pl.ds(at, 2), :] * has_north
        return carry

    lax.fori_loop(0, lons, fill, 0)
    for f in range(fields):
        west[pl.ds(f * 2 * span, 2 * span), :] = ring_out[pl.ds(f * ring + 2 * span, 2 * span), :]
        east[pl.ds(f * 2 * span, 2 * span), :] = ring_out[
            pl.ds(f * ring + lons * span, 2 * span), :
        ]


def widen(coef, south, north):
    fields, lons, lats, _ = coef.shape
    span = lats + 4
    vm = pl.BlockSpec(memory_space=V)
    edge = V((fields * 2 * span, LANES), jnp.float32)
    return pl.pallas_call(
        widen_kernel,
        out_shape=(V((fields * (lons + 4) * span, LANES), jnp.float32), edge, edge),
        in_specs=[pl.BlockSpec(memory_space=pltpu.HBM), vm, vm],
        out_specs=(vm, vm, vm),
        scratch_shapes=[V(coef.shape, jnp.float32), pltpu.SemaphoreType.DMA],
        compiler_params=params(),
        name="widen",
    )(in_hbm(coef), in_vmem(south), in_vmem(north))


def combine_kernel(lons, lats, ring_ref, west, east, out_ref, field):
    me = lax.axis_index("lat")
    total = lats * lax.axis_size("lat")
    span, rim = lats + 4, lats + 2
    ring = (lons + 4) * span
    size = rim_rows(lons, lats)
    field[...] = ring_ref[...]
    for f in range(field.shape[0] // ring):
        field[pl.ds(f * ring, 2 * span), :] = west[pl.ds(f * 2 * span, 2 * span), :]
        field[pl.ds(f * ring + (lons + 2) * span, 2 * span), :] = east[
            pl.ds(f * 2 * span, 2 * span), :
        ]
    lev = lax.broadcasted_iota(jnp.int32, (8, LANES), 1)
    row = lax.broadcasted_iota(jnp.int32, (8, LANES), 0)

    def one(i, carry):
        for r in chunks(rim):
            lat = row + (r - 1) + me * lats
            inside = (lat >= 0) & (lat < total)
            at = (i + 1) * span + r + 1

            def wind(f, shift, at=at):
                return ADVECT_SCALE * field[pl.ds(f * ring + at + shift, 8), :]

            def half(shift, at=at):
                return 0.5 * field[pl.ds(2 * ring + at + shift, 8), :]

            mine = half(0)
            east_factor = wind(0, 0) + (mine + half(span))
            west_factor = (mine + half(-span)) - wind(0, -span)
            north_factor = wind(1, 0) + (mine + half(1))
            south_factor = (mine + half(-1)) - wind(1, -1)
            up = jnp.where(lev < LANES - 1, mine + pltpu.roll(mine, LANES - 1, 1), 0.0)
            down = jnp.where(lev > 0, mine + pltpu.roll(mine, 1, 1), 0.0)
            centre = 1.0 - (
                ((east_factor + west_factor) + (north_factor + south_factor)) + (up + down)
            )
            factors = (centre, east_factor, west_factor, north_factor, south_factor, up, down)
            for k, value in enumerate(factors):
                out_ref[pl.ds(k * size + i * rim + r, 8), :] = jnp.where(inside, value, 0.0)
        return carry

    lax.fori_loop(0, lons + 2, one, 0)


def combine(ring, west, east, lons, lats):
    vm = pl.BlockSpec(memory_space=V)
    return pl.pallas_call(
        functools.partial(combine_kernel, lons, lats),
        out_shape=V((7 * rim_rows(lons, lats), LANES), jnp.float32),
        in_specs=[vm, vm, vm],
        out_specs=vm,
        scratch_shapes=[V(ring.shape, jnp.float32)],
        compiler_params=params(),
        name="combine",
    )(in_vmem(ring), in_vmem(west), in_vmem(east))


def rim_rows(lons, lats):
    return -(-(lons + 2) * (lats + 2) // 8) * 8


def chunks(rows):
    starts = list(range(0, rows - 7, 8))
    if starts[-1] + 8 < rows:
        starts.append(rows - 8)
    return starts


def weighted(factors, source, at, east):
    centre = source[pl.ds(at, 8), :]
    total = factors[0] * centre + factors[1] * source[pl.ds(at + east, 8), :]
    other = factors[2] * source[pl.ds(at - east, 8), :] + factors[3] * source[pl.ds(at + 1, 8), :]
    third = factors[4] * source[pl.ds(at - 1, 8), :] + factors[5] * pltpu.roll(
        centre, LANES - 1, 1
    )
    return (total + other) + (third + factors[6] * pltpu.roll(centre, 1, 1))


def first_step(coef_ref, state, mid, nv, lons, lats, i):
    span, rim = lats + 4, lats + 2
    ring, size = (lons + 4) * span, rim_rows(lons, lats)
    for r in chunks(rim):
        factors = [coef_ref[pl.ds(k * size + i * rim + r, 8), :] for k in range(7)]
        for v in range(nv):
            mid[pl.ds(v * size + i * rim + r, 8), :] = weighted(
                factors, state, v * ring + (i + 1) * span + r + 1, span
            )


def second_step(coef_ref, mid, out, nv, lons, lats, i, place):
    rim = lats + 2
    size = rim_rows(lons, lats)
    for r in range(0, lats, 8):
        at = (i + 1) * rim + r + 1
        factors = [coef_ref[pl.ds(k * size + at, 8), :] for k in range(7)]
        for v in range(nv):
            out[pl.ds(pl.multiple_of(place(v) + r, 8), 8), :] = weighted(
                factors, mid, v * size + at, rim
            )


def insert_kernel(lons, lats, state_in, south, north, state, west, east):
    span = lats + 4
    ring = (lons + 4) * span
    nv = state.shape[0] // ring

    def strip(i, carry):
        for v in range(nv):
            at = v * ring + (i + 2) * span
            frm = (v * lons + i) * 2
            state[pl.ds(at, 2), :] = south[pl.ds(frm, 2), :]
            state[pl.ds(at + lats + 2, 2), :] = north[pl.ds(frm, 2), :]
        return carry

    lax.fori_loop(0, lons, strip, 0)
    for v in range(nv):
        west[pl.ds(v * 2 * span, 2 * span), :] = state[pl.ds(v * ring + 2 * span, 2 * span), :]
        east[pl.ds(v * 2 * span, 2 * span), :] = state[pl.ds(v * ring + lons * span, 2 * span), :]


def insert(state, south, north, shape):
    nv, lons, lats = shape
    vm = pl.BlockSpec(memory_space=V)
    edge = V((nv * 2 * (lats + 4), LANES), jnp.float32)
    return pl.pallas_call(
        functools.partial(insert_kernel, lons, lats),
        out_shape=(V(state.shape, jnp.float32), edge, edge),
        in_specs=[vm] * 3,
        out_specs=(vm,) * 3,
        input_output_aliases={0: 0},
        compiler_params=params(),
        name="insert",
    )(in_vmem(state), in_vmem(south), in_vmem(north))


def inner_kernel(lons, lats, coef_ref, state, mid, out_ref, out, sem):
    nv = out.shape[0] // (lons * lats)
    cells = lons * lats

    def first(i, carry):
        first_step(coef_ref, state, mid, nv, lons, lats, i)
        return carry

    lax.fori_loop(2, lons, first, 0)

    def second(i, carry):
        second_step(
            coef_ref, mid, out, nv, lons, lats, i, lambda v: v * cells + i * lats
        )
        return carry

    parts = 4
    edges = [2 + (lons - 4) * p // parts for p in range(parts + 1)]
    copies = []
    for p in range(parts):
        lax.fori_loop(edges[p], edges[p + 1], second, 0)
        for v in range(nv):
            span = pl.ds(v * cells + edges[p] * lats, (edges[p + 1] - edges[p]) * lats)
            copy = pltpu.make_async_copy(out.at[span], out_ref.at[span], sem.at[p * nv + v])
            copy.start()
            copies.append(copy)
    wait_all(copies)


def inner(coef, state, shape):
    nv, lons, lats = shape
    vm = pl.BlockSpec(memory_space=V)
    return pl.pallas_call(
        functools.partial(inner_kernel, lons, lats),
        out_shape=(
            V((nv * rim_rows(lons, lats), LANES), jnp.float32),
            jax.ShapeDtypeStruct((nv * lons * lats, LANES), jnp.float32),
        ),
        in_specs=[vm, vm],
        out_specs=(vm, pl.BlockSpec(memory_space=pltpu.HBM)),
        scratch_shapes=[
            V((nv * lons * lats, LANES), jnp.float32),
            pltpu.SemaphoreType.DMA((4 * nv,)),
        ],
        compiler_params=params(),
        name="inner",
    )(in_vmem(coef), in_vmem(state))


def outer_kernel(
    lons, lats, coef_ref, state_in, mid_in, west, east, out_in, state, mid, out_ref, out, sem
):
    span = lats + 4
    ring = (lons + 4) * span
    nv = state.shape[0] // ring
    cells = lons * lats
    for v in range(nv):
        state[pl.ds(v * ring, 2 * span), :] = west[pl.ds(v * 2 * span, 2 * span), :]
        state[pl.ds(v * ring + (lons + 2) * span, 2 * span), :] = east[
            pl.ds(v * 2 * span, 2 * span), :
        ]

    def first(k, carry):
        i = jnp.where(k < 2, k, lons - 2 + k)
        first_step(coef_ref, state, mid, nv, lons, lats, i)
        return carry

    lax.fori_loop(0, 4, first, 0)

    def second(k, carry):
        i = jnp.where(k < 2, k, lons - 4 + k)
        second_step(
            coef_ref, mid, out, nv, lons, lats, i, lambda v: (v * 4 + k) * lats
        )
        return carry

    lax.fori_loop(0, 4, second, 0)
    copies = []
    for v in range(nv):
        for side, at in ((0, 0), (1, lons - 2)):
            copies.append(
                pltpu.make_async_copy(
                    out.at[pl.ds((v * 4 + 2 * side) * lats, 2 * lats)],
                    out_ref.at[pl.ds(v * cells + at * lats, 2 * lats)],
                    sem.at[v * 2 + side],
                )
            )
    run(copies)


def outer(coef, state, mid, west, east, out, shape):
    nv, lons, lats = shape
    vm = pl.BlockSpec(memory_space=V)
    hbm = pl.BlockSpec(memory_space=pltpu.HBM)
    return pl.pallas_call(
        functools.partial(outer_kernel, lons, lats),
        out_shape=(
            V(state.shape, jnp.float32),
            V(mid.shape, jnp.float32),
            jax.ShapeDtypeStruct(out.shape, jnp.float32),
        ),
        in_specs=[vm] * 5 + [hbm],
        out_specs=(vm, vm, hbm),
        input_output_aliases={1: 0, 2: 1, 5: 2},
        scratch_shapes=[V((nv * 4 * lats, LANES), jnp.float32), pltpu.SemaphoreType.DMA((2 * nv,))],
        compiler_params=params(),
        name="outer",
    )(in_vmem(coef), in_vmem(state), in_vmem(mid), in_vmem(west), in_vmem(east), out)[2]


def from_sides(low_part, high_part, axis, periodic):
    count = lax.axis_size(axis)
    forward = [(i, i + 1) for i in range(count - 1)]
    if periodic:
        forward.append((count - 1, 0))
    backward = [(target, source) for source, target in forward]
    return lax.ppermute(high_part, axis, forward), lax.ppermute(low_part, axis, backward)


def body(
    adjoint_in, departures, obs_band, obs_station, obs_var, counts, station_cell, coefficients
):
    nv, lons, lats, levels = adjoint_in.shape
    shape = (nv, lons, lats)
    slots = departures.shape[2]
    n = lax.axis_size("lat")
    cap = -(-3 * slots // n // 8) * 8
    stations = station_cell.shape[2]
    square = (slots // LANES, LANES)
    own, swap, *rest = pack(
        n,
        cap,
        stations,
        counts,
        obs_band.reshape(square),
        obs_station.reshape(square),
        obs_var.reshape(square),
        departures.reshape(slots, levels),
        coefficients,
    )
    through, (south, north) = rest[:-2], rest[-2:]
    swapped = lax.ppermute(swap, "lat", [(i, i ^ 1) for i in range(n)])
    south, north = from_sides(south, north, "lat", False)
    through = relay(swapped, through, cap + HEADER)
    order = sorted(range(1, n // 2), key=lambda s: abs(4 * s - n))
    moved = [
        lax.ppermute(through[s - 1], "lat", [(i, (i + 2 * s) % n) for i in range(n)])
        for s in order
    ]
    cell = station_cell.reshape(1, stations)
    span = lats + 4
    spot = (cell // lats + 2) * span + cell % lats + 2
    tile = (lons + 4) * span
    table = jnp.concatenate([spot + v * tile for v in range(nv)], axis=1)
    state = scatter_first(
        table, adjoint_in.reshape(nv * lons * lats, levels), own, swapped, cap, shape
    )
    ring, west, east = widen(coefficients, south, north)
    west, east = from_sides(west, east, "lon", True)
    coef = combine(ring, west, east, lons, lats)
    state = scatter_more(table, state, moved[:1], cap, shape, False, (coef,))
    state, south, north = scatter_more(table, state, moved[1:], cap, shape, True)
    south, north = from_sides(south, north, "lat", False)
    state, west, east = insert(state, south, north, shape)
    west, east = from_sides(west, east, "lon", True)
    mid, out = inner(coef, state, shape)
    out = outer(coef, state, mid, west, east, out, shape)
    return out.reshape(adjoint_in.shape)


def solution(mesh):
    in_specs = (
        P(None, "lon", "lat", None),
        P("lon", "lat", None, None),
        P("lon", "lat", None, None),
        P("lon", "lat", None),
        P("lon", "lat", None),
        P("lon", "lat"),
        P("lon", "lat", None),
        P(None, "lon", "lat", None),
    )
    out_specs = P(None, "lon", "lat", None)
    return jax.shard_map(body, mesh=mesh, in_specs=in_specs, out_specs=out_specs, check_vma=False)
```

```python
import functools

import jax
import jax.numpy as jnp
from jax import lax
from jax.experimental import pallas as pl
from jax.experimental.pallas import tpu as pltpu
from jax.sharding import PartitionSpec as P

ADVECT_SCALE = 0.2
LANES = 128
STRIDE = 1024
HEADER = 8
VMEM_LIMIT = 40 * 1024 * 1024
V = pltpu.VMEM


def in_vmem(array):
    return pltpu.with_memory_space_constraint(array, V)


def in_hbm(array):
    return pltpu.with_memory_space_constraint(array, pltpu.HBM)


def params():
    return pltpu.CompilerParams(vmem_limit_bytes=VMEM_LIMIT)


def start_all(copies):
    for copy in copies:
        copy.start()


def wait_all(copies):
    for copy in copies:
        copy.wait()


def run(copies):
    start_all(copies)
    wait_all(copies)


def pairs_of(axis, periodic):
    count = lax.axis_size(axis)
    near = [(i, i ^ 1) for i in range(count)]
    across = []
    for i in range(1, count, 2):
        if periodic or i + 1 < count:
            across += [(i, (i + 1) % count), ((i + 1) % count, i)]
    return near, across


def swap_sides(near, across, axis, periodic):
    near_pairs, across_pairs = pairs_of(axis, periodic)
    return lax.ppermute(near, axis, near_pairs), lax.ppermute(across, axis, across_pairs)


def near_side(low, high, axis="lat"):
    odd = (lax.axis_index(axis) & 1) == 1
    return jnp.where(odd, low, high), jnp.where(odd, high, low)


def pack_kernel(
    n, cap, stations, count_ref, band_ref, station_ref, var_ref, dep_ref, coef_ref, *rest
):
    half = n // 2
    own, swap = rest[:2]
    through = rest[2 : half + 1]
    near, across = rest[half + 1 : half + 3]
    (dep, band, station, var, edge, buf, pos_v, pos_s, sem) = rest[half + 3 :]
    me = lax.axis_index("lat")
    rows, lanes = band.shape
    lat_cells = coef_ref.shape[2]
    loads = [
        pltpu.make_async_copy(src, dst, sem.at[k])
        for k, (src, dst) in enumerate(
            (
                (band_ref, band),
                (station_ref, station),
                (var_ref, var),
                (dep_ref, dep),
                (coef_ref.at[:, :, pl.ds(0, 8)], edge.at[0]),
                (coef_ref.at[:, :, pl.ds(lat_cells - 8, 8)], edge.at[1]),
            )
        )
    ]
    start_all(loads)
    wait_all(loads[:3])
    count = count_ref[0, 0]
    slot = (
        lax.broadcasted_iota(jnp.int32, (rows, lanes), 0) * lanes
        + lax.broadcasted_iota(jnp.int32, (rows, lanes), 1)
    )
    far = (band[...] >> 1) - (me >> 1)
    far = jnp.where(far < 0, far + half, far)
    group = jnp.where((band[...] & 1) == (me & 1), far, far + half)
    group = jnp.where(slot < count, group, n)
    masks = jnp.concatenate([(group == s).astype(jnp.float32) for s in range(n)], axis=0)
    before = lax.broadcasted_iota(jnp.int32, (lanes, lanes), 0) < lax.broadcasted_iota(
        jnp.int32, (lanes, lanes), 1
    )
    prefix = jnp.dot(masks, before.astype(jnp.float32), preferred_element_type=jnp.float32)
    totals = jnp.dot(
        masks, jnp.ones((lanes, lanes), jnp.float32), preferred_element_type=jnp.float32
    )
    a = lax.broadcasted_iota(jnp.int32, (rows * n, rows * n), 0)
    b = lax.broadcasted_iota(jnp.int32, (rows * n, rows * n), 1)
    earlier = ((a // rows == b // rows) & (b < a)).astype(jnp.float32)
    offset = jnp.dot(earlier, totals, preferred_element_type=jnp.float32)
    ranks = (prefix + offset).astype(jnp.int32)
    rank = jnp.zeros((rows, lanes), jnp.int32)
    for s in range(n):
        rank = jnp.where(group == s, ranks[s * rows : (s + 1) * rows], rank)
    pos_v[...] = group * STRIDE + rank
    place_map = pltpu.make_async_copy(pos_v, pos_s, sem.at[0])
    place_map.start()
    code = var[...] * stations + station[...]
    upper = (code >> 6).astype(jnp.float32)
    lower = (code & 63).astype(jnp.float32)
    width = -(-cap // lanes) * lanes
    which = lax.broadcasted_iota(jnp.int32, (n, lanes), 0)
    order = lax.broadcasted_iota(jnp.int32, (width, lanes), 0)
    codes = jnp.zeros((2 * n, width), jnp.float32)
    for k in range(rows):
        mine = which == group[k : k + 1]
        parts = jnp.concatenate(
            [jnp.where(mine, upper[k : k + 1], 0.0), jnp.where(mine, lower[k : k + 1], 0.0)], 0
        )
        codes += lax.dot_general(
            parts,
            (order == rank[k : k + 1]).astype(jnp.float32),
            (((1,), (1,)), ((), ())),
            preferred_element_type=jnp.float32,
        )
    codes = codes[:n] * 64.0 + codes[n:]
    counts = offset + totals
    size = cap + HEADER

    def target(s):
        if s == 0:
            return own, 0
        if s < half:
            return through[s - 1], 0
        return swap, (s - half) * size

    for s in range(n):
        to, at = target(s)
        for j in range(width // lanes):
            to[pl.ds(at + cap + j, 1), :] = codes[s : s + 1, j * lanes : (j + 1) * lanes]
        to[pl.ds(at + cap + HEADER - 1, 1), :] = counts[(s + 1) * rows - 1 : (s + 1) * rows]
    wait_all(loads[3:])
    fields, lons = edge.shape[1:3]
    odd = me & 1

    def strip(i, carry):
        for f in range(fields):
            near[pl.ds((f * lons + i) * 2, 2), :] = edge[1 - odd, f, i, pl.ds(6 - 6 * odd, 2), :]
            across[pl.ds((f * lons + i) * 2, 2), :] = edge[odd, f, i, pl.ds(6 * odd, 2), :]
        return carry

    lax.fori_loop(0, lons, strip, 0)
    place_map.wait()

    def place(g, carry):
        base = pl.multiple_of(g * 16, 16)
        row, col = base >> 7, base & 127
        for k in range(16):
            buf[pl.ds(pos_s[row, col + k], 1), :] = dep[pl.ds(base + k, 1), :]
        return carry

    lax.fori_loop(0, (count + 15) >> 4, place, 0)
    for s in range(n):
        to, at = target(s)
        to[pl.ds(at, cap), :] = buf[pl.ds(s * STRIDE, cap), :]


def pack(n, cap, stations, count, band, station, var, dep, coef):
    rows = dep.shape[0] // LANES
    fields, lons = coef.shape[:2]
    size, half = cap + HEADER, n // 2
    strip = (fields * lons * 2, LANES)
    shapes = [(size, LANES), (half * size, LANES)]
    shapes += [(2 * size, LANES)] * (half - 1) + [strip, strip]
    hbm = pl.BlockSpec(memory_space=pltpu.HBM)
    vm = pl.BlockSpec(memory_space=V)
    return pl.pallas_call(
        functools.partial(pack_kernel, n, cap, stations),
        out_shape=tuple(V(shape, jnp.float32) for shape in shapes),
        in_specs=[pl.BlockSpec(memory_space=pltpu.SMEM)] + [hbm] * 5,
        out_specs=(vm,) * len(shapes),
        scratch_shapes=[
            V(dep.shape, jnp.float32),
            V((rows, LANES), jnp.int32),
            V((rows, LANES), jnp.int32),
            V((rows, LANES), jnp.int32),
            V((2, fields, lons, 8, LANES), jnp.float32),
            V((n * STRIDE + HEADER + STRIDE, LANES), jnp.float32),
            V((rows, LANES), jnp.int32),
            pltpu.SMEM((rows, LANES), jnp.int32),
            pltpu.SemaphoreType.DMA((6,)),
        ],
        compiler_params=params(),
        name="pack",
    )(count, *(in_hbm(array) for array in (band, station, var, dep, coef)))


def relay_kernel(shifts, size, swapped, *rest):
    for s, to in zip(shifts, rest[len(rest) - len(shifts) :]):
        to[pl.ds(size, size), :] = swapped[pl.ds(s * size, size), :]


def relay(swapped, through, shifts, size, after=()):
    k = len(shifts)
    vm = pl.BlockSpec(memory_space=V)
    picked = [through[s - 1] for s in shifts]
    return pl.pallas_call(
        functools.partial(relay_kernel, shifts, size),
        out_shape=tuple(V(array.shape, jnp.float32) for array in picked),
        in_specs=[vm] * (k + 1 + len(after)),
        out_specs=(vm,) * k,
        input_output_aliases={j + 1: j for j in range(k)},
        compiler_params=params(),
        name="relay",
    )(in_vmem(swapped), *(in_vmem(array) for array in (*picked, *after)))


def open_header(packet, base, cap, view, header, sem):
    view[...] = packet[pl.ds(base + cap, HEADER), :].astype(jnp.int32)
    copy = pltpu.make_async_copy(view, header, sem)
    copy.start()
    return copy


def scatter_packet(table_ref, packet, start, header, state):
    unroll = 8
    count = header[HEADER - 1, 0]

    def some(g, carry):
        base = g * unroll
        major, minor = base >> 7, base & 127
        rows = [table_ref[0, header[major, minor + k]] for k in range(unroll)]
        for k in range(unroll):
            state[pl.ds(rows[k], 1), :] += packet[pl.ds(start + base + k, 1), :]
        return carry

    def one(j, carry):
        row = table_ref[0, header[j >> 7, j & 127]]
        state[pl.ds(row, 1), :] += packet[pl.ds(start + j, 1), :]
        return carry

    whole = count >> 3
    lax.fori_loop(0, whole, some, 0)
    lax.fori_loop(whole * unroll, count, one, 0)


def first_kernel(
    lons, lats, cap, table_ref, adjoint_ref, own_ref, swap_ref, state, full, *rest
):
    views, headers, sem = rest[:2], rest[2:4], rest[4]
    span = lats + 4
    ring = (lons + 4) * span
    nv = state.shape[0] // ring
    load = pltpu.make_async_copy(adjoint_ref, full, sem.at[0])
    load.start()
    packets = (own_ref, swap_ref)
    opened = [
        open_header(packets[j], 0, cap, views[j], headers[j], sem.at[j + 1]) for j in range(2)
    ]
    load.wait()

    def fill(i, carry):
        for v in range(nv):
            to = v * ring + (i + 2) * span + 2
            at = (v * lons + i) * lats
            for r in range(0, lats, 8):
                state[pl.ds(to + r, 8), :] = full[pl.ds(pl.multiple_of(at + r, 8), 8), :]
        return carry

    lax.fori_loop(0, lons, fill, 0)
    wait_all(opened)
    for j in range(2):
        scatter_packet(table_ref, packets[j], 0, headers[j], state)


def scatter_first(table, adjoint, own, swapped, cap, shape):
    nv, lons, lats = shape
    hbm = pl.BlockSpec(memory_space=pltpu.HBM)
    ring = (lons + 4) * (lats + 4)
    return pl.pallas_call(
        functools.partial(first_kernel, lons, lats, cap),
        out_shape=V((nv * ring, LANES), jnp.float32),
        in_specs=[pl.BlockSpec(memory_space=pltpu.SMEM), hbm] + [pl.BlockSpec(memory_space=V)] * 2,
        out_specs=pl.BlockSpec(memory_space=V),
        scratch_shapes=[
            V(adjoint.shape, jnp.float32),
            V((HEADER, LANES), jnp.int32),
            V((HEADER, LANES), jnp.int32),
            pltpu.SMEM((HEADER, LANES), jnp.int32),
            pltpu.SMEM((HEADER, LANES), jnp.int32),
            pltpu.SemaphoreType.DMA((3,)),
        ],
        compiler_params=params(),
        name="scatter_own",
    )(table, in_hbm(adjoint), in_vmem(own), in_vmem(swapped))


def more_kernel(k, lons, lats, cap, last, table_ref, *rest):
    packets = [(rest[j], base) for j in range(k) for base in (0, cap + HEADER)]
    m = len(packets)
    rest = rest[len(rest) - (3 if last else 1) - 2 * m - 1 :]
    outs, rest = rest[: 3 if last else 1], rest[3 if last else 1 :]
    views, headers, sem = rest[:m], rest[m : 2 * m], rest[2 * m]
    state = outs[0]
    opened = [
        open_header(*packets[j], cap, views[j], headers[j], sem.at[j]) for j in range(m)
    ]
    wait_all(opened)
    for j in range(m):
        scatter_packet(table_ref, *packets[j], headers[j], state)
    if not last:
        return
    near, across = outs[1:]
    span = lats + 4
    ring = (lons + 4) * span
    nv = state.shape[0] // ring
    near_row, across_row = near_side(2, lats)

    def strip(i, carry):
        for v in range(nv):
            at = v * ring + (i + 2) * span
            to = (v * lons + i) * 2
            near[pl.ds(to, 2), :] = state[pl.ds(at + near_row, 2), :]
            across[pl.ds(to, 2), :] = state[pl.ds(at + across_row, 2), :]
        return carry

    lax.fori_loop(0, lons, strip, 0)


def scatter_more(table, state, packets, cap, shape, last, after=()):
    nv, lons, lats = shape
    k = len(packets)
    vm = pl.BlockSpec(memory_space=V)
    out = V(state.shape, jnp.float32)
    strip = V((nv * lons * 2, LANES), jnp.float32)
    return pl.pallas_call(
        functools.partial(more_kernel, k, lons, lats, cap, last),
        out_shape=(out, strip, strip) if last else out,
        in_specs=[pl.BlockSpec(memory_space=pltpu.SMEM)] + [vm] * (k + 1 + len(after)),
        out_specs=(vm, vm, vm) if last else vm,
        input_output_aliases={k + 1: 0},
        scratch_shapes=[V((HEADER, LANES), jnp.int32)] * (2 * k)
        + [pltpu.SMEM((HEADER, LANES), jnp.int32)] * (2 * k)
        + [pltpu.SemaphoreType.DMA((2 * k,))],
        compiler_params=params(),
        name="scatter_last" if last else "scatter_more",
    )(
        table,
        *(in_vmem(packet) for packet in packets),
        in_vmem(state),
        *(in_vmem(array) for array in after),
    )


def widen_kernel(coef_ref, near_ref, across_ref, after, ring_out, near_lon, across_lon, own, sem):
    fields, lons, lats, _ = coef_ref.shape
    span = lats + 4
    ring = (lons + 4) * span
    near_row, across_row = near_side(0, lats + 2)
    near_at, across_at = near_side(2 * span, lons * span, "lon")
    run([pltpu.make_async_copy(coef_ref, own, sem)])

    def fill(i, carry):
        for f in range(fields):
            to = f * ring + (i + 2) * span
            at = (f * lons + i) * 2
            for r in range(0, lats, 8):
                ring_out[pl.ds(to + 2 + r, 8), :] = own[f, i, r : r + 8]
            ring_out[pl.ds(to + near_row, 2), :] = near_ref[pl.ds(at, 2), :]
            ring_out[pl.ds(to + across_row, 2), :] = across_ref[pl.ds(at, 2), :]
        return carry

    lax.fori_loop(0, lons, fill, 0)
    take_lons(ring_out, near_lon, across_lon, fields, ring, 2 * span, near_at, across_at)


def take_lons(ring_ref, near, across, count, ring, size, near_at, across_at):
    for f in range(count):
        near[pl.ds(f * size, size), :] = ring_ref[pl.ds(f * ring + near_at, size), :]
        across[pl.ds(f * size, size), :] = ring_ref[pl.ds(f * ring + across_at, size), :]


def put_lons(ring_ref, near, across, count, ring, size, near_at, across_at):
    for f in range(count):
        ring_ref[pl.ds(f * ring + near_at, size), :] = near[pl.ds(f * size, size), :]
        ring_ref[pl.ds(f * ring + across_at, size), :] = across[pl.ds(f * size, size), :]


def widen(coef, near, across, after):
    fields, lons, lats, _ = coef.shape
    span = lats + 4
    vm = pl.BlockSpec(memory_space=V)
    edge = V((fields * 2 * span, LANES), jnp.float32)
    return pl.pallas_call(
        widen_kernel,
        out_shape=(V((fields * (lons + 4) * span, LANES), jnp.float32), edge, edge),
        in_specs=[pl.BlockSpec(memory_space=pltpu.HBM), vm, vm, vm],
        out_specs=(vm, vm, vm),
        scratch_shapes=[V(coef.shape, jnp.float32), pltpu.SemaphoreType.DMA],
        compiler_params=params(),
        name="widen",
    )(in_hbm(coef), in_vmem(near), in_vmem(across), in_vmem(after))


def combine_kernel(lons, lats, ring_ref, near, across, out_ref, field):
    me = lax.axis_index("lat")
    total = lats * lax.axis_size("lat")
    span, rim = lats + 4, lats + 2
    ring = (lons + 4) * span
    size = rim_rows(lons, lats)
    field[...] = ring_ref[...]
    ends = near_side(0, (lons + 2) * span, "lon")
    put_lons(field, near, across, field.shape[0] // ring, ring, 2 * span, *ends)
    lev = lax.broadcasted_iota(jnp.int32, (8, LANES), 1)
    row = lax.broadcasted_iota(jnp.int32, (8, LANES), 0)

    def one(i, carry):
        for r in chunks(rim):
            lat = row + (r - 1) + me * lats
            inside = (lat >= 0) & (lat < total)
            at = (i + 1) * span + r + 1

            def wind(f, shift, at=at):
                return ADVECT_SCALE * field[pl.ds(f * ring + at + shift, 8), :]

            def half(shift, at=at):
                return 0.5 * field[pl.ds(2 * ring + at + shift, 8), :]

            mine = half(0)
            east_factor = wind(0, 0) + (mine + half(span))
            west_factor = (mine + half(-span)) - wind(0, -span)
            north_factor = wind(1, 0) + (mine + half(1))
            south_factor = (mine + half(-1)) - wind(1, -1)
            up = jnp.where(lev < LANES - 1, mine + pltpu.roll(mine, LANES - 1, 1), 0.0)
            down = jnp.where(lev > 0, mine + pltpu.roll(mine, 1, 1), 0.0)
            centre = 1.0 - (
                ((east_factor + west_factor) + (north_factor + south_factor)) + (up + down)
            )
            factors = (centre, east_factor, west_factor, north_factor, south_factor, up, down)
            for k, value in enumerate(factors):
                out_ref[pl.ds(k * size + i * rim + r, 8), :] = jnp.where(inside, value, 0.0)
        return carry

    lax.fori_loop(0, lons + 2, one, 0)


def combine(ring, near, across, lons, lats):
    vm = pl.BlockSpec(memory_space=V)
    return pl.pallas_call(
        functools.partial(combine_kernel, lons, lats),
        out_shape=V((7 * rim_rows(lons, lats), LANES), jnp.float32),
        in_specs=[vm, vm, vm],
        out_specs=vm,
        scratch_shapes=[V(ring.shape, jnp.float32)],
        compiler_params=params(),
        name="combine",
    )(in_vmem(ring), in_vmem(near), in_vmem(across))


def rim_rows(lons, lats):
    return -(-(lons + 2) * (lats + 2) // 8) * 8


def chunks(rows):
    starts = list(range(0, rows - 7, 8))
    if starts[-1] + 8 < rows:
        starts.append(rows - 8)
    return starts


def weighted(factors, source, at, east, rows=None):
    rows = rows or (lambda start: pl.ds(start, 8))
    centre = source[rows(at), :]
    total = factors[0] * centre + factors[1] * source[rows(at + east), :]
    other = factors[2] * source[rows(at - east), :] + factors[3] * source[rows(at + 1), :]
    third = factors[4] * source[rows(at - 1), :] + factors[5] * pltpu.roll(centre, LANES - 1, 1)
    return (total + other) + (third + factors[6] * pltpu.roll(centre, 1, 1))


def first_step(coef_ref, state, mid, nv, lons, lats, i, starts):
    span, rim = lats + 4, lats + 2
    ring, size = (lons + 4) * span, rim_rows(lons, lats)
    for r in starts:
        factors = [coef_ref[pl.ds(k * size + i * rim + r, 8), :] for k in range(7)]
        for v in range(nv):
            mid[pl.ds(v * size + i * rim + r, 8), :] = weighted(
                factors, state, v * ring + (i + 1) * span + r + 1, span
            )


def first_step_along(coef_ref, state, mid, nv, lons, lats, i, r):
    span, rim = lats + 4, lats + 2
    ring, size = (lons + 4) * span, rim_rows(lons, lats)

    def rim_at(start):
        return pl.ds(start, 8, stride=rim)

    def ring_at(start):
        return pl.ds(start, 8, stride=span)

    factors = [coef_ref[rim_at(k * size + i * rim + r), :] for k in range(7)]
    for v in range(nv):
        mid[rim_at(v * size + i * rim + r), :] = weighted(
            factors, state, v * ring + (i + 1) * span + r + 1, span, ring_at
        )


def second_step(coef_ref, mid, out, nv, lons, lats, i, place):
    rim = lats + 2
    size = rim_rows(lons, lats)
    for r in range(0, lats, 8):
        at = (i + 1) * rim + r + 1
        factors = [coef_ref[pl.ds(k * size + at, 8), :] for k in range(7)]
        for v in range(nv):
            out[pl.ds(pl.multiple_of(place(v) + r, 8), 8), :] = weighted(
                factors, mid, v * size + at, rim
            )


def insert_kernel(lons, lats, state_in, near, across, state, near_lon, across_lon):
    span = lats + 4
    ring = (lons + 4) * span
    nv = state.shape[0] // ring

    near_row, across_row = near_side(0, lats + 2)

    def strip(i, carry):
        for v in range(nv):
            at = v * ring + (i + 2) * span
            frm = (v * lons + i) * 2
            state[pl.ds(at + near_row, 2), :] = near[pl.ds(frm, 2), :]
            state[pl.ds(at + across_row, 2), :] = across[pl.ds(frm, 2), :]
        return carry

    lax.fori_loop(0, lons, strip, 0)
    ends = near_side(2 * span, lons * span, "lon")
    take_lons(state, near_lon, across_lon, nv, ring, 2 * span, *ends)


def insert(state, near, across, shape):
    nv, lons, lats = shape
    vm = pl.BlockSpec(memory_space=V)
    edge = V((nv * 2 * (lats + 4), LANES), jnp.float32)
    return pl.pallas_call(
        functools.partial(insert_kernel, lons, lats),
        out_shape=(V(state.shape, jnp.float32), edge, edge),
        in_specs=[vm] * 3,
        out_specs=(vm,) * 3,
        input_output_aliases={0: 0},
        compiler_params=params(),
        name="insert",
    )(in_vmem(state), in_vmem(near), in_vmem(across))


def early_kernel(nv, lons, lats, coef_ref, state, mid):
    starts = [r + 2 for r in chunks(lats - 2)]

    def first(i, carry):
        first_step(coef_ref, state, mid, nv, lons, lats, i, starts)
        return carry

    lax.fori_loop(2, lons, first, 0)


def early(coef, state, shape):
    nv, lons, lats = shape
    vm = pl.BlockSpec(memory_space=V)
    return pl.pallas_call(
        functools.partial(early_kernel, nv, lons, lats),
        out_shape=V((nv * rim_rows(lons, lats), LANES), jnp.float32),
        in_specs=[vm, vm],
        out_specs=vm,
        compiler_params=params(),
        name="early",
    )(in_vmem(coef), in_vmem(state))


def inner_kernel(lons, lats, coef_ref, state, mid_in, mid, out_ref, out, sem):
    nv = out.shape[0] // (lons * lats)
    cells = lons * lats
    for r in (0, 1, lats, lats + 1):

        def first(k, carry, r=r):
            i = jnp.minimum(2 + 8 * k, lons - 8)
            first_step_along(coef_ref, state, mid, nv, lons, lats, i, r)
            return carry

        lax.fori_loop(0, -(-(lons - 2) // 8), first, 0)

    def second(i, carry):
        second_step(
            coef_ref, mid, out, nv, lons, lats, i, lambda v: v * cells + i * lats
        )
        return carry

    parts = 4
    edges = [2 + (lons - 4) * p // parts for p in range(parts + 1)]
    copies = []
    for p in range(parts):
        lax.fori_loop(edges[p], edges[p + 1], second, 0)
        for v in range(nv):
            span = pl.ds(v * cells + edges[p] * lats, (edges[p + 1] - edges[p]) * lats)
            copy = pltpu.make_async_copy(out.at[span], out_ref.at[span], sem.at[p * nv + v])
            copy.start()
            copies.append(copy)
    wait_all(copies)


def inner(coef, state, mid, shape):
    nv, lons, lats = shape
    vm = pl.BlockSpec(memory_space=V)
    return pl.pallas_call(
        functools.partial(inner_kernel, lons, lats),
        out_shape=(
            V(mid.shape, jnp.float32),
            jax.ShapeDtypeStruct((nv * lons * lats, LANES), jnp.float32),
        ),
        in_specs=[vm, vm, vm],
        out_specs=(vm, pl.BlockSpec(memory_space=pltpu.HBM)),
        input_output_aliases={2: 0},
        scratch_shapes=[
            V((nv * lons * lats, LANES), jnp.float32),
            pltpu.SemaphoreType.DMA((4 * nv,)),
        ],
        compiler_params=params(),
        name="inner",
    )(in_vmem(coef), in_vmem(state), in_vmem(mid))


def outer_kernel(
    lons, lats, coef_ref, state_in, mid_in, near, across, out_in, state, mid, out_ref, out, sem
):
    span = lats + 4
    ring = (lons + 4) * span
    nv = state.shape[0] // ring
    cells = lons * lats
    ends = near_side(0, (lons + 2) * span, "lon")
    put_lons(state, near, across, nv, ring, 2 * span, *ends)

    def first(k, carry):
        i = jnp.where(k < 2, k, lons - 2 + k)
        first_step(coef_ref, state, mid, nv, lons, lats, i, chunks(lats + 2))
        return carry

    lax.fori_loop(0, 4, first, 0)

    def second(k, carry):
        i = jnp.where(k < 2, k, lons - 4 + k)
        second_step(
            coef_ref, mid, out, nv, lons, lats, i, lambda v: (v * 4 + k) * lats
        )
        return carry

    lax.fori_loop(0, 4, second, 0)
    copies = []
    for v in range(nv):
        for side, at in ((0, 0), (1, lons - 2)):
            copies.append(
                pltpu.make_async_copy(
                    out.at[pl.ds((v * 4 + 2 * side) * lats, 2 * lats)],
                    out_ref.at[pl.ds(v * cells + at * lats, 2 * lats)],
                    sem.at[v * 2 + side],
                )
            )
    run(copies)


def outer(coef, state, mid, near, across, out, shape):
    nv, lons, lats = shape
    vm = pl.BlockSpec(memory_space=V)
    hbm = pl.BlockSpec(memory_space=pltpu.HBM)
    return pl.pallas_call(
        functools.partial(outer_kernel, lons, lats),
        out_shape=(
            V(state.shape, jnp.float32),
            V(mid.shape, jnp.float32),
            jax.ShapeDtypeStruct(out.shape, jnp.float32),
        ),
        in_specs=[vm] * 5 + [hbm],
        out_specs=(vm, vm, hbm),
        input_output_aliases={1: 0, 2: 1, 5: 2},
        scratch_shapes=[V((nv * 4 * lats, LANES), jnp.float32), pltpu.SemaphoreType.DMA((2 * nv,))],
        compiler_params=params(),
        name="outer",
    )(in_vmem(coef), in_vmem(state), in_vmem(mid), in_vmem(near), in_vmem(across), out)[2]


def body(
    adjoint_in, departures, obs_band, obs_station, obs_var, counts, station_cell, coefficients
):
    nv, lons, lats, levels = adjoint_in.shape
    shape = (nv, lons, lats)
    slots = departures.shape[2]
    n = lax.axis_size("lat")
    cap = -(-3 * slots // n // 8) * 8
    stations = station_cell.shape[2]
    square = (slots // LANES, LANES)
    own, swap, *rest = pack(
        n,
        cap,
        stations,
        counts,
        obs_band.reshape(square),
        obs_station.reshape(square),
        obs_var.reshape(square),
        departures.reshape(slots, levels),
        coefficients,
    )
    through, (near, across) = rest[:-2], rest[-2:]
    swapped = lax.ppermute(swap, "lat", [(i, i ^ 1) for i in range(n)])
    near, across = swap_sides(near, across, "lat", False)
    size = cap + HEADER
    order = sorted(range(1, n // 2), key=lambda s: abs(4 * s - n))
    cell = station_cell.reshape(1, stations)
    span = lats + 4
    spot = (cell // lats + 2) * span + cell % lats + 2
    tile = (lons + 4) * span
    table = jnp.concatenate([spot + v * tile for v in range(nv)], axis=1)
    def send(shifts, after):
        return [
            lax.ppermute(packet, "lat", [(i, (i + 2 * s) % n) for i in range(n)])
            for s, packet in zip(shifts, relay(swapped, through, shifts, size, after))
        ]

    middle = 1 + (len(order) - 1) // 2
    first = relay(swapped, through, order[:1], size)
    moved = [lax.ppermute(first[0], "lat", [(i, (i + 2 * order[0]) % n) for i in range(n)])]
    state = scatter_first(
        table, adjoint_in.reshape(nv * lons * lats, levels), own, swapped, cap, shape
    )
    second = send(order[1:middle], (state,))
    ring, near, across = widen(coefficients, near, across, state)
    third = send(order[middle:], (ring,))
    near, across = swap_sides(near, across, "lon", True)
    coef = combine(ring, near, across, lons, lats)
    state = scatter_more(table, state, moved, cap, shape, False)
    state, near, across = scatter_more(table, state, second + third, cap, shape, True, (coef,))
    near, across = swap_sides(near, across, "lat", False)
    mid = early(coef, state, shape)
    state, near, across = insert(state, near, across, shape)
    near, across = swap_sides(near, across, "lon", True)
    mid, out = inner(coef, state, mid, shape)
    out = outer(coef, state, mid, near, across, out, shape)
    return out.reshape(adjoint_in.shape)


def solution(mesh):
    in_specs = (
        P(None, "lon", "lat", None),
        P("lon", "lat", None, None),
        P("lon", "lat", None, None),
        P("lon", "lat", None),
        P("lon", "lat", None),
        P("lon", "lat"),
        P("lon", "lat", None),
        P(None, "lon", "lat", None),
    )
    out_specs = P(None, "lon", "lat", None)
    return jax.shard_map(body, mesh=mesh, in_specs=in_specs, out_specs=out_specs, check_vma=False)
```

```python
import functools

import jax
import jax.numpy as jnp
from jax import lax
from jax.experimental import pallas as pl
from jax.experimental.pallas import tpu as pltpu
from jax.sharding import PartitionSpec as P

ADVECT_SCALE = 0.2
LANES = 128
STRIDE = 1024
HEADER = 8
VMEM_LIMIT = 40 * 1024 * 1024
V = pltpu.VMEM


def in_vmem(array):
    return pltpu.with_memory_space_constraint(array, V)


def in_hbm(array):
    return pltpu.with_memory_space_constraint(array, pltpu.HBM)


def params():
    return pltpu.CompilerParams(vmem_limit_bytes=VMEM_LIMIT)


def start_all(copies):
    for copy in copies:
        copy.start()


def wait_all(copies):
    for copy in copies:
        copy.wait()


def run(copies):
    start_all(copies)
    wait_all(copies)


def pairs_of(axis, periodic):
    count = lax.axis_size(axis)
    near = [(i, i ^ 1) for i in range(count)]
    across = []
    for i in range(1, count, 2):
        if periodic or i + 1 < count:
            across += [(i, (i + 1) % count), ((i + 1) % count, i)]
    return near, across


def swap_sides(near, across, axis, periodic):
    near_pairs, across_pairs = pairs_of(axis, periodic)
    return lax.ppermute(near, axis, near_pairs), lax.ppermute(across, axis, across_pairs)


def near_side(low, high, axis="lat"):
    odd = (lax.axis_index(axis) & 1) == 1
    return jnp.where(odd, low, high), jnp.where(odd, high, low)


def pack_kernel(
    n, cap, stations, count_ref, band_ref, station_ref, var_ref, dep_ref, coef_ref, *rest
):
    half = n // 2
    own, swap = rest[:2]
    through = rest[2 : half + 1]
    near, across = rest[half + 1 : half + 3]
    (dep, band, station, var, edge, buf, pos_v, pos_s, sem) = rest[half + 3 :]
    me = lax.axis_index("lat")
    rows, lanes = band.shape
    lat_cells = coef_ref.shape[2]
    loads = [
        pltpu.make_async_copy(src, dst, sem.at[k])
        for k, (src, dst) in enumerate(
            (
                (band_ref, band),
                (station_ref, station),
                (var_ref, var),
                (dep_ref, dep),
                (coef_ref.at[:, :, pl.ds(0, 8)], edge.at[0]),
                (coef_ref.at[:, :, pl.ds(lat_cells - 8, 8)], edge.at[1]),
            )
        )
    ]
    start_all(loads)
    wait_all(loads[:3])
    count = count_ref[0, 0]
    slot = (
        lax.broadcasted_iota(jnp.int32, (rows, lanes), 0) * lanes
        + lax.broadcasted_iota(jnp.int32, (rows, lanes), 1)
    )
    far = (band[...] >> 1) - (me >> 1)
    far = jnp.where(far < 0, far + half, far)
    group = jnp.where((band[...] & 1) == (me & 1), far, far + half)
    group = jnp.where(slot < count, group, n)
    masks = jnp.concatenate([(group == s).astype(jnp.float32) for s in range(n)], axis=0)
    before = lax.broadcasted_iota(jnp.int32, (lanes, lanes), 0) < lax.broadcasted_iota(
        jnp.int32, (lanes, lanes), 1
    )
    prefix = jnp.dot(masks, before.astype(jnp.float32), preferred_element_type=jnp.float32)
    totals = jnp.dot(
        masks, jnp.ones((lanes, lanes), jnp.float32), preferred_element_type=jnp.float32
    )
    a = lax.broadcasted_iota(jnp.int32, (rows * n, rows * n), 0)
    b = lax.broadcasted_iota(jnp.int32, (rows * n, rows * n), 1)
    earlier = ((a // rows == b // rows) & (b < a)).astype(jnp.float32)
    offset = jnp.dot(earlier, totals, preferred_element_type=jnp.float32)
    ranks = (prefix + offset).astype(jnp.int32)
    rank = jnp.zeros((rows, lanes), jnp.int32)
    for s in range(n):
        rank = jnp.where(group == s, ranks[s * rows : (s + 1) * rows], rank)
    pos_v[...] = group * STRIDE + rank
    place_map = pltpu.make_async_copy(pos_v, pos_s, sem.at[0])
    place_map.start()
    code = var[...] * stations + station[...]
    upper = (code >> 6).astype(jnp.float32)
    lower = (code & 63).astype(jnp.float32)
    width = -(-cap // lanes) * lanes
    which = lax.broadcasted_iota(jnp.int32, (n, lanes), 0)
    order = lax.broadcasted_iota(jnp.int32, (width, lanes), 0)
    codes = jnp.zeros((2 * n, width), jnp.float32)
    for k in range(rows):
        mine = which == group[k : k + 1]
        parts = jnp.concatenate(
            [jnp.where(mine, upper[k : k + 1], 0.0), jnp.where(mine, lower[k : k + 1], 0.0)], 0
        )
        codes += lax.dot_general(
            parts,
            (order == rank[k : k + 1]).astype(jnp.float32),
            (((1,), (1,)), ((), ())),
            preferred_element_type=jnp.float32,
        )
    codes = codes[:n] * 64.0 + codes[n:]
    counts = offset + totals
    size = cap + HEADER

    def target(s):
        if s == 0:
            return own, 0
        if s < half:
            return through[s - 1], 0
        return swap, (s - half) * size

    for s in range(n):
        to, at = target(s)
        for j in range(width // lanes):
            to[pl.ds(at + cap + j, 1), :] = codes[s : s + 1, j * lanes : (j + 1) * lanes]
        to[pl.ds(at + cap + HEADER - 1, 1), :] = counts[(s + 1) * rows - 1 : (s + 1) * rows]
    wait_all(loads[3:])
    fields, lons = edge.shape[1:3]
    odd = me & 1

    def strip(i, carry):
        for f in range(fields):
            near[pl.ds((f * lons + i) * 2, 2), :] = edge[1 - odd, f, i, pl.ds(6 - 6 * odd, 2), :]
            across[pl.ds((f * lons + i) * 2, 2), :] = edge[odd, f, i, pl.ds(6 * odd, 2), :]
        return carry

    lax.fori_loop(0, lons, strip, 0)
    place_map.wait()

    def place(g, carry):
        base = pl.multiple_of(g * 16, 16)
        row, col = base >> 7, base & 127
        for k in range(16):
            buf[pl.ds(pos_s[row, col + k], 1), :] = dep[pl.ds(base + k, 1), :]
        return carry

    lax.fori_loop(0, (count + 15) >> 4, place, 0)
    for s in range(n):
        to, at = target(s)
        to[pl.ds(at, cap), :] = buf[pl.ds(s * STRIDE, cap), :]


def pack(n, cap, stations, count, band, station, var, dep, coef):
    rows = dep.shape[0] // LANES
    fields, lons = coef.shape[:2]
    size, half = cap + HEADER, n // 2
    strip = (fields * lons * 2, LANES)
    shapes = [(size, LANES), (half * size, LANES)]
    shapes += [
        (size if s == half // 2 else 2 * size, LANES) for s in range(1, half)
    ] + [strip, strip]
    hbm = pl.BlockSpec(memory_space=pltpu.HBM)
    vm = pl.BlockSpec(memory_space=V)
    return pl.pallas_call(
        functools.partial(pack_kernel, n, cap, stations),
        out_shape=tuple(V(shape, jnp.float32) for shape in shapes),
        in_specs=[pl.BlockSpec(memory_space=pltpu.SMEM)] + [hbm] * 5,
        out_specs=(vm,) * len(shapes),
        scratch_shapes=[
            V(dep.shape, jnp.float32),
            V((rows, LANES), jnp.int32),
            V((rows, LANES), jnp.int32),
            V((rows, LANES), jnp.int32),
            V((2, fields, lons, 8, LANES), jnp.float32),
            V((n * STRIDE + HEADER + STRIDE, LANES), jnp.float32),
            V((rows, LANES), jnp.int32),
            pltpu.SMEM((rows, LANES), jnp.int32),
            pltpu.SemaphoreType.DMA((6,)),
        ],
        compiler_params=params(),
        name="pack",
    )(count, *(in_hbm(array) for array in (band, station, var, dep, coef)))


def relay_kernel(shifts, size, swapped, *rest):
    for s, to in zip(shifts, rest[len(rest) - len(shifts) :]):
        to[pl.ds(size, size), :] = swapped[pl.ds(s * size, size), :]


def relay(swapped, through, shifts, size, after=()):
    k = len(shifts)
    vm = pl.BlockSpec(memory_space=V)
    picked = [through[s - 1] for s in shifts]
    return pl.pallas_call(
        functools.partial(relay_kernel, shifts, size),
        out_shape=tuple(V(array.shape, jnp.float32) for array in picked),
        in_specs=[vm] * (k + 1 + len(after)),
        out_specs=(vm,) * k,
        input_output_aliases={j + 1: j for j in range(k)},
        compiler_params=params(),
        name="relay",
    )(in_vmem(swapped), *(in_vmem(array) for array in (*picked, *after)))


def alone_kernel(start, swapped, *rest):
    to = rest[-1]
    to[...] = swapped[pl.ds(start, to.shape[0]), :]


def alone(swapped, s, size, after=()):
    vm = pl.BlockSpec(memory_space=V)
    return pl.pallas_call(
        functools.partial(alone_kernel, s * size),
        out_shape=V((size, LANES), jnp.float32),
        in_specs=[vm] * (1 + len(after)),
        out_specs=vm,
        compiler_params=params(),
        name="alone",
    )(in_vmem(swapped), *(in_vmem(array) for array in after))


def open_header(packet, base, cap, view, header, sem):
    view[...] = packet[pl.ds(base + cap, HEADER), :].astype(jnp.int32)
    copy = pltpu.make_async_copy(view, header, sem)
    copy.start()
    return copy


def scatter_packet(table_ref, packet, start, header, state):
    unroll = 8
    count = header[HEADER - 1, 0]

    def some(g, carry):
        base = g * unroll
        major, minor = base >> 7, base & 127
        rows = [table_ref[0, header[major, minor + k]] for k in range(unroll)]
        for k in range(unroll):
            state[pl.ds(rows[k], 1), :] += packet[pl.ds(start + base + k, 1), :]
        return carry

    def one(j, carry):
        row = table_ref[0, header[j >> 7, j & 127]]
        state[pl.ds(row, 1), :] += packet[pl.ds(start + j, 1), :]
        return carry

    whole = count >> 3
    lax.fori_loop(0, whole, some, 0)
    lax.fori_loop(whole * unroll, count, one, 0)


def first_kernel(
    k, lons, lats, cap, table_ref, adjoint_ref, *rest
):
    packets, (state, full) = rest[:k], rest[len(rest) - 2 * k - 3 : len(rest) - 2 * k - 1]
    rest = rest[len(rest) - 2 * k - 1 :]
    views, headers, sem = rest[:k], rest[k : 2 * k], rest[2 * k]
    span = lats + 4
    ring = (lons + 4) * span
    nv = state.shape[0] // ring
    load = pltpu.make_async_copy(adjoint_ref, full, sem.at[0])
    load.start()
    opened = [
        open_header(packets[j], 0, cap, views[j], headers[j], sem.at[j + 1]) for j in range(k)
    ]
    load.wait()

    def fill(i, carry):
        for v in range(nv):
            to = v * ring + (i + 2) * span + 2
            at = (v * lons + i) * lats
            for r in range(0, lats, 8):
                state[pl.ds(to + r, 8), :] = full[pl.ds(pl.multiple_of(at + r, 8), 8), :]
        return carry

    lax.fori_loop(0, lons, fill, 0)
    wait_all(opened)
    for j in range(k):
        scatter_packet(table_ref, packets[j], 0, headers[j], state)


def scatter_first(table, adjoint, packets, cap, shape, after=()):
    nv, lons, lats = shape
    k = len(packets)
    hbm = pl.BlockSpec(memory_space=pltpu.HBM)
    ring = (lons + 4) * (lats + 4)
    return pl.pallas_call(
        functools.partial(first_kernel, k, lons, lats, cap),
        out_shape=V((nv * ring, LANES), jnp.float32),
        in_specs=[pl.BlockSpec(memory_space=pltpu.SMEM), hbm]
        + [pl.BlockSpec(memory_space=V)] * (k + len(after)),
        out_specs=pl.BlockSpec(memory_space=V),
        scratch_shapes=[
            V(adjoint.shape, jnp.float32),
            *[V((HEADER, LANES), jnp.int32)] * k,
            *[pltpu.SMEM((HEADER, LANES), jnp.int32)] * k,
            pltpu.SemaphoreType.DMA((k + 1,)),
        ],
        compiler_params=params(),
        name="scatter_own",
    )(table, in_hbm(adjoint), *(in_vmem(array) for array in (*packets, *after)))


def more_kernel(k, lons, lats, cap, last, table_ref, *rest):
    size = cap + HEADER
    packets = [(rest[j], base) for j in range(k) for base in range(0, rest[j].shape[0], size)]
    m = len(packets)
    rest = rest[len(rest) - (3 if last else 1) - 2 * m - 1 :]
    outs, rest = rest[: 3 if last else 1], rest[3 if last else 1 :]
    views, headers, sem = rest[:m], rest[m : 2 * m], rest[2 * m]
    state = outs[0]
    opened = [
        open_header(*packets[j], cap, views[j], headers[j], sem.at[j]) for j in range(m)
    ]
    wait_all(opened)
    for j in range(m):
        scatter_packet(table_ref, *packets[j], headers[j], state)
    if not last:
        return
    near, across = outs[1:]
    span = lats + 4
    ring = (lons + 4) * span
    nv = state.shape[0] // ring
    near_row, across_row = near_side(2, lats)

    def strip(i, carry):
        for v in range(nv):
            at = v * ring + (i + 2) * span
            to = (v * lons + i) * 2
            near[pl.ds(to, 2), :] = state[pl.ds(at + near_row, 2), :]
            across[pl.ds(to, 2), :] = state[pl.ds(at + across_row, 2), :]
        return carry

    lax.fori_loop(0, lons, strip, 0)


def scatter_more(table, state, packets, cap, shape, last, after=()):
    nv, lons, lats = shape
    k = len(packets)
    m = sum(packet.shape[0] // (cap + HEADER) for packet in packets)
    vm = pl.BlockSpec(memory_space=V)
    out = V(state.shape, jnp.float32)
    strip = V((nv * lons * 2, LANES), jnp.float32)
    return pl.pallas_call(
        functools.partial(more_kernel, k, lons, lats, cap, last),
        out_shape=(out, strip, strip) if last else out,
        in_specs=[pl.BlockSpec(memory_space=pltpu.SMEM)] + [vm] * (k + 1 + len(after)),
        out_specs=(vm, vm, vm) if last else vm,
        input_output_aliases={k + 1: 0},
        scratch_shapes=[V((HEADER, LANES), jnp.int32)] * m
        + [pltpu.SMEM((HEADER, LANES), jnp.int32)] * m
        + [pltpu.SemaphoreType.DMA((m,))],
        compiler_params=params(),
        name="scatter_last" if last else "scatter_more",
    )(
        table,
        *(in_vmem(packet) for packet in packets),
        in_vmem(state),
        *(in_vmem(array) for array in after),
    )


def widen_kernel(coef_ref, near_ref, across_ref, after, ring_out, near_lon, across_lon, own, sem):
    fields, lons, lats, _ = coef_ref.shape
    span = lats + 4
    ring = (lons + 4) * span
    near_row, across_row = near_side(0, lats + 2)
    near_at, across_at = near_side(2 * span, lons * span, "lon")
    run([pltpu.make_async_copy(coef_ref, own, sem)])

    def fill(i, carry):
        for f in range(fields):
            to = f * ring + (i + 2) * span
            at = (f * lons + i) * 2
            for r in range(0, lats, 8):
                ring_out[pl.ds(to + 2 + r, 8), :] = own[f, i, r : r + 8]
            ring_out[pl.ds(to + near_row, 2), :] = near_ref[pl.ds(at, 2), :]
            ring_out[pl.ds(to + across_row, 2), :] = across_ref[pl.ds(at, 2), :]
        return carry

    lax.fori_loop(0, lons, fill, 0)
    take_lons(ring_out, near_lon, across_lon, fields, ring, 2 * span, near_at, across_at)


def take_lons(ring_ref, near, across, count, ring, size, near_at, across_at):
    for f in range(count):
        near[pl.ds(f * size, size), :] = ring_ref[pl.ds(f * ring + near_at, size), :]
        across[pl.ds(f * size, size), :] = ring_ref[pl.ds(f * ring + across_at, size), :]


def put_lons(ring_ref, near, across, count, ring, size, near_at, across_at):
    for f in range(count):
        ring_ref[pl.ds(f * ring + near_at, size), :] = near[pl.ds(f * size, size), :]
        ring_ref[pl.ds(f * ring + across_at, size), :] = across[pl.ds(f * size, size), :]


def widen(coef, near, across, after):
    fields, lons, lats, _ = coef.shape
    span = lats + 4
    vm = pl.BlockSpec(memory_space=V)
    edge = V((fields * 2 * span, LANES), jnp.float32)
    return pl.pallas_call(
        widen_kernel,
        out_shape=(V((fields * (lons + 4) * span, LANES), jnp.float32), edge, edge),
        in_specs=[pl.BlockSpec(memory_space=pltpu.HBM), vm, vm, vm],
        out_specs=(vm, vm, vm),
        scratch_shapes=[V(coef.shape, jnp.float32), pltpu.SemaphoreType.DMA],
        compiler_params=params(),
        name="widen",
    )(in_hbm(coef), in_vmem(near), in_vmem(across), in_vmem(after))


def combine_kernel(lons, lats, ring_ref, near, across, out_ref, field):
    me = lax.axis_index("lat")
    total = lats * lax.axis_size("lat")
    span, rim = lats + 4, lats + 2
    ring = (lons + 4) * span
    size = rim_rows(lons, lats)
    field[...] = ring_ref[...]
    ends = near_side(0, (lons + 2) * span, "lon")
    put_lons(field, near, across, field.shape[0] // ring, ring, 2 * span, *ends)
    lev = lax.broadcasted_iota(jnp.int32, (8, LANES), 1)
    row = lax.broadcasted_iota(jnp.int32, (8, LANES), 0)

    def one(i, carry):
        for r in chunks(rim):
            lat = row + (r - 1) + me * lats
            inside = (lat >= 0) & (lat < total)
            at = (i + 1) * span + r + 1

            def wind(f, shift, at=at):
                return ADVECT_SCALE * field[pl.ds(f * ring + at + shift, 8), :]

            def half(shift, at=at):
                return 0.5 * field[pl.ds(2 * ring + at + shift, 8), :]

            mine = half(0)
            east_factor = wind(0, 0) + (mine + half(span))
            west_factor = (mine + half(-span)) - wind(0, -span)
            north_factor = wind(1, 0) + (mine + half(1))
            south_factor = (mine + half(-1)) - wind(1, -1)
            up = jnp.where(lev < LANES - 1, mine + pltpu.roll(mine, LANES - 1, 1), 0.0)
            down = jnp.where(lev > 0, mine + pltpu.roll(mine, 1, 1), 0.0)
            centre = 1.0 - (
                ((east_factor + west_factor) + (north_factor + south_factor)) + (up + down)
            )
            factors = (centre, east_factor, west_factor, north_factor, south_factor, up, down)
            for k, value in enumerate(factors):
                out_ref[pl.ds(k * size + i * rim + r, 8), :] = jnp.where(inside, value, 0.0)
        return carry

    lax.fori_loop(0, lons + 2, one, 0)


def combine(ring, near, across, lons, lats):
    vm = pl.BlockSpec(memory_space=V)
    return pl.pallas_call(
        functools.partial(combine_kernel, lons, lats),
        out_shape=V((7 * rim_rows(lons, lats), LANES), jnp.float32),
        in_specs=[vm, vm, vm],
        out_specs=vm,
        scratch_shapes=[V(ring.shape, jnp.float32)],
        compiler_params=params(),
        name="combine",
    )(in_vmem(ring), in_vmem(near), in_vmem(across))


def rim_rows(lons, lats):
    return -(-(lons + 2) * (lats + 2) // 8) * 8


def chunks(rows):
    starts = list(range(0, rows - 7, 8))
    if starts[-1] + 8 < rows:
        starts.append(rows - 8)
    return starts


def shift_matrix():
    k = lax.broadcasted_iota(jnp.int32, (2 * LANES, 2 * LANES), 0) & (LANES - 1)
    j = lax.broadcasted_iota(jnp.int32, (2 * LANES, 2 * LANES), 1)
    take = ((j < LANES) & (k == j + 1)) | ((j >= LANES) & (k == j - LANES - 1))
    return take.astype(jnp.float32).astype(jnp.bfloat16)


def shifted(centres, matrix):
    block = jnp.concatenate(centres, axis=0)
    high = block.astype(jnp.bfloat16)
    low = (block - high.astype(jnp.float32)).astype(jnp.bfloat16)
    both = jnp.dot(
        jnp.concatenate([high, low], axis=1), matrix, preferred_element_type=jnp.float32
    )
    return [
        (both[8 * k : 8 * k + 8, :LANES], both[8 * k : 8 * k + 8, LANES:])
        for k in range(len(centres))
    ]


def rolled(centre):
    return pltpu.roll(centre, LANES - 1, 1), pltpu.roll(centre, 1, 1)


def weighted(factors, source, at, east, rows=None, levels=None):
    rows = rows or (lambda start: pl.ds(start, 8))
    centre = source[rows(at), :]
    above, below = levels or rolled(centre)
    total = factors[0] * centre + factors[1] * source[rows(at + east), :]
    other = factors[2] * source[rows(at - east), :] + factors[3] * source[rows(at + 1), :]
    third = factors[4] * source[rows(at - 1), :] + factors[5] * above
    return (total + other) + (third + factors[6] * below)


def step_rows(coef_ref, source, nv, spots, stride, east, put, matrix):
    size = coef_ref.shape[0] // 7
    levels = [None] * (len(spots) * nv)
    if matrix is not None:
        part = int(len(levels) * 0.5) // 2 * 2
        levels[:part] = shifted(
            [source[pl.ds(v * stride + at, 8), :] for _, at in spots for v in range(nv)][:part],
            matrix,
        )
    for k, (row, at) in enumerate(spots):
        factors = [coef_ref[pl.ds(f * size + row, 8), :] for f in range(7)]
        for v in range(nv):
            put(
                k,
                v,
                weighted(
                    factors, source, v * stride + at, east, levels=levels[k * nv + v]
                ),
            )


def first_step(coef_ref, state, mid, nv, lons, lats, places, starts, matrix=None):
    span, rim = lats + 4, lats + 2
    ring, size = (lons + 4) * span, rim_rows(lons, lats)
    spots = [(i * rim + r, (i + 1) * span + r + 1) for i in places for r in starts]

    def put(k, v, value):
        mid[pl.ds(v * size + spots[k][0], 8), :] = value

    step_rows(coef_ref, state, nv, spots, ring, span, put, matrix)


def first_step_along(coef_ref, state, mid, nv, lons, lats, i, r):
    span, rim = lats + 4, lats + 2
    ring, size = (lons + 4) * span, rim_rows(lons, lats)

    def rim_at(start):
        return pl.ds(start, 8, stride=rim)

    def ring_at(start):
        return pl.ds(start, 8, stride=span)

    factors = [coef_ref[rim_at(k * size + i * rim + r), :] for k in range(7)]
    for v in range(nv):
        mid[rim_at(v * size + i * rim + r), :] = weighted(
            factors, state, v * ring + (i + 1) * span + r + 1, span, ring_at
        )


def second_step(coef_ref, mid, out, nv, lons, lats, places, place, matrix=None):
    rim = lats + 2
    spots = [
        ((i + 1) * rim + r + 1, (i + 1) * rim + r + 1) for i in places for r in range(0, lats, 8)
    ]
    each = lats // 8

    def put(k, v, value):
        at = place(v, k // each) + (k % each) * 8
        out[pl.ds(pl.multiple_of(at, 8), 8), :] = value

    step_rows(coef_ref, mid, nv, spots, rim_rows(lons, lats), rim, put, matrix)


def insert_kernel(lons, lats, state_in, near, across, state, near_lon, across_lon):
    span = lats + 4
    ring = (lons + 4) * span
    nv = state.shape[0] // ring

    near_row, across_row = near_side(0, lats + 2)

    def strip(i, carry):
        for v in range(nv):
            at = v * ring + (i + 2) * span
            frm = (v * lons + i) * 2
            state[pl.ds(at + near_row, 2), :] = near[pl.ds(frm, 2), :]
            state[pl.ds(at + across_row, 2), :] = across[pl.ds(frm, 2), :]
        return carry

    lax.fori_loop(0, lons, strip, 0)
    ends = near_side(2 * span, lons * span, "lon")
    take_lons(state, near_lon, across_lon, nv, ring, 2 * span, *ends)


def insert(state, near, across, shape):
    nv, lons, lats = shape
    vm = pl.BlockSpec(memory_space=V)
    edge = V((nv * 2 * (lats + 4), LANES), jnp.float32)
    return pl.pallas_call(
        functools.partial(insert_kernel, lons, lats),
        out_shape=(V(state.shape, jnp.float32), edge, edge),
        in_specs=[vm] * 3,
        out_specs=(vm,) * 3,
        input_output_aliases={0: 0},
        compiler_params=params(),
        name="insert",
    )(in_vmem(state), in_vmem(near), in_vmem(across))


def early_kernel(nv, lons, lats, coef_ref, state, mid):
    starts = [r + 2 for r in chunks(lats - 2)]
    matrix = shift_matrix()

    def first(i, carry):
        first_step(
            coef_ref, state, mid, nv, lons, lats, (2 + 2 * i, 3 + 2 * i), starts, matrix
        )
        return carry

    lax.fori_loop(0, (lons - 2) // 2, first, 0)


def early(coef, state, shape):
    nv, lons, lats = shape
    vm = pl.BlockSpec(memory_space=V)
    return pl.pallas_call(
        functools.partial(early_kernel, nv, lons, lats),
        out_shape=V((nv * rim_rows(lons, lats), LANES), jnp.float32),
        in_specs=[vm, vm],
        out_specs=vm,
        compiler_params=params(),
        name="early",
    )(in_vmem(coef), in_vmem(state))


def inner_kernel(lons, lats, coef_ref, state, mid_in, mid, out_ref, out, sem):
    nv = out.shape[0] // (lons * lats)
    cells = lons * lats
    for r in (0, 1, lats, lats + 1):

        def first(k, carry, r=r):
            i = jnp.minimum(2 + 8 * k, lons - 8)
            first_step_along(coef_ref, state, mid, nv, lons, lats, i, r)
            return carry

        lax.fori_loop(0, -(-(lons - 2) // 8), first, 0)

    matrix = shift_matrix()

    def second(i, carry):
        second_step(
            coef_ref,
            mid,
            out,
            nv,
            lons,
            lats,
            (2 * i, 2 * i + 1),
            lambda v, k: v * cells + (2 * i + k) * lats,
            matrix,
        )
        return carry

    parts = 4
    edges = [2 + (lons - 4) // 2 * p // parts * 2 for p in range(parts + 1)]
    copies = []
    for p in range(parts):
        lax.fori_loop(edges[p] // 2, edges[p + 1] // 2, second, 0)
        for v in range(nv):
            span = pl.ds(v * cells + edges[p] * lats, (edges[p + 1] - edges[p]) * lats)
            copy = pltpu.make_async_copy(out.at[span], out_ref.at[span], sem.at[p * nv + v])
            copy.start()
            copies.append(copy)
    wait_all(copies)


def inner(coef, state, mid, shape):
    nv, lons, lats = shape
    vm = pl.BlockSpec(memory_space=V)
    return pl.pallas_call(
        functools.partial(inner_kernel, lons, lats),
        out_shape=(
            V(mid.shape, jnp.float32),
            jax.ShapeDtypeStruct((nv * lons * lats, LANES), jnp.float32),
        ),
        in_specs=[vm, vm, vm],
        out_specs=(vm, pl.BlockSpec(memory_space=pltpu.HBM)),
        input_output_aliases={2: 0},
        scratch_shapes=[
            V((nv * lons * lats, LANES), jnp.float32),
            pltpu.SemaphoreType.DMA((4 * nv,)),
        ],
        compiler_params=params(),
        name="inner",
    )(in_vmem(coef), in_vmem(state), in_vmem(mid))


def outer_kernel(
    lons, lats, coef_ref, state_in, mid_in, near, across, out_in, state, mid, out_ref, out, sem
):
    span = lats + 4
    ring = (lons + 4) * span
    nv = state.shape[0] // ring
    cells = lons * lats
    ends = near_side(0, (lons + 2) * span, "lon")
    put_lons(state, near, across, nv, ring, 2 * span, *ends)

    def first(k, carry):
        i = jnp.where(k < 2, k, lons - 2 + k)
        first_step(coef_ref, state, mid, nv, lons, lats, (i,), chunks(lats + 2))
        return carry

    lax.fori_loop(0, 4, first, 0)

    def second(k, carry):
        i = jnp.where(k < 2, k, lons - 4 + k)
        second_step(
            coef_ref, mid, out, nv, lons, lats, (i,), lambda v, _: (v * 4 + k) * lats
        )
        return carry

    lax.fori_loop(0, 4, second, 0)
    copies = []
    for v in range(nv):
        for side, at in ((0, 0), (1, lons - 2)):
            copies.append(
                pltpu.make_async_copy(
                    out.at[pl.ds((v * 4 + 2 * side) * lats, 2 * lats)],
                    out_ref.at[pl.ds(v * cells + at * lats, 2 * lats)],
                    sem.at[v * 2 + side],
                )
            )
    run(copies)


def outer(coef, state, mid, near, across, out, shape):
    nv, lons, lats = shape
    vm = pl.BlockSpec(memory_space=V)
    hbm = pl.BlockSpec(memory_space=pltpu.HBM)
    return pl.pallas_call(
        functools.partial(outer_kernel, lons, lats),
        out_shape=(
            V(state.shape, jnp.float32),
            V(mid.shape, jnp.float32),
            jax.ShapeDtypeStruct(out.shape, jnp.float32),
        ),
        in_specs=[vm] * 5 + [hbm],
        out_specs=(vm, vm, hbm),
        input_output_aliases={1: 0, 2: 1, 5: 2},
        scratch_shapes=[V((nv * 4 * lats, LANES), jnp.float32), pltpu.SemaphoreType.DMA((2 * nv,))],
        compiler_params=params(),
        name="outer",
    )(in_vmem(coef), in_vmem(state), in_vmem(mid), in_vmem(near), in_vmem(across), out)[2]


def body(
    adjoint_in, departures, obs_band, obs_station, obs_var, counts, station_cell, coefficients
):
    nv, lons, lats, levels = adjoint_in.shape
    shape = (nv, lons, lats)
    slots = departures.shape[2]
    n = lax.axis_size("lat")
    cap = -(-3 * slots // n // 8) * 8
    stations = station_cell.shape[2]
    square = (slots // LANES, LANES)
    own, swap, *rest = pack(
        n,
        cap,
        stations,
        counts,
        obs_band.reshape(square),
        obs_station.reshape(square),
        obs_var.reshape(square),
        departures.reshape(slots, levels),
        coefficients,
    )
    through, (near, across) = rest[:-2], rest[-2:]
    swapped = lax.ppermute(swap, "lat", [(i, i ^ 1) for i in range(n)])
    near, across = swap_sides(near, across, "lat", False)
    size = cap + HEADER
    order = sorted(range(1, n // 2), key=lambda s: abs(4 * s - n))
    cell = station_cell.reshape(1, stations)
    span = lats + 4
    spot = (cell // lats + 2) * span + cell % lats + 2
    tile = (lons + 4) * span
    table = jnp.concatenate([spot + v * tile for v in range(nv)], axis=1)
    def send(s, packet):
        return lax.ppermute(packet, "lat", [(i, (i + 2 * s) % n) for i in range(n)])

    def send_pairs(shifts, after):
        return [
            send(s, packet)
            for s, packet in zip(shifts, relay(swapped, through, shifts, size, after))
        ]

    middle = 1 + (len(order) - 1) // 2
    adjoint = adjoint_in.reshape(nv * lons * lats, levels)
    ahead = send(order[0], through[order[0] - 1])
    second = send_pairs(order[1:middle], ())
    ring, near, across = widen(coefficients, near, across, swapped)
    third = send_pairs(order[middle:], (ring,))
    near, across = swap_sides(near, across, "lon", True)
    coef = combine(ring, near, across, lons, lats)
    state = scatter_first(table, adjoint, [own, swapped, ahead], cap, shape, (coef,))
    moved = [send(order[0], alone(swapped, order[0], size, (state,)))]
    state = scatter_more(table, state, second, cap, shape, False)
    state = scatter_more(table, state, third, cap, shape, False)
    state, near, across = scatter_more(table, state, moved, cap, shape, True)
    near, across = swap_sides(near, across, "lat", False)
    mid = early(coef, state, shape)
    state, near, across = insert(state, near, across, shape)
    near, across = swap_sides(near, across, "lon", True)
    mid, out = inner(coef, state, mid, shape)
    out = outer(coef, state, mid, near, across, out, shape)
    return out.reshape(adjoint_in.shape)


def solution(mesh):
    in_specs = (
        P(None, "lon", "lat", None),
        P("lon", "lat", None, None),
        P("lon", "lat", None, None),
        P("lon", "lat", None),
        P("lon", "lat", None),
        P("lon", "lat"),
        P("lon", "lat", None),
        P(None, "lon", "lat", None),
    )
    out_specs = P(None, "lon", "lat", None)
    return jax.shard_map(body, mesh=mesh, in_specs=in_specs, out_specs=out_specs, check_vma=False)
```

```python
import functools

import jax
import jax.numpy as jnp
from jax import lax
from jax.experimental import pallas as pl
from jax.experimental.pallas import tpu as pltpu
from jax.sharding import PartitionSpec as P

ADVECT_SCALE = 0.2
LANES = 128
GROUP = 4
STRIDE = 1024
HEADER = 8
VMEM_LIMIT = 40 * 1024 * 1024
V = pltpu.VMEM


def in_vmem(array):
    return pltpu.with_memory_space_constraint(array, V)


def in_hbm(array):
    return pltpu.with_memory_space_constraint(array, pltpu.HBM)


def params():
    return pltpu.CompilerParams(vmem_limit_bytes=VMEM_LIMIT)


def start_all(copies):
    for copy in copies:
        copy.start()


def wait_all(copies):
    for copy in copies:
        copy.wait()


def run(copies):
    start_all(copies)
    wait_all(copies)


def pairs_of(axis, periodic):
    count = lax.axis_size(axis)
    near = [(i, i ^ 1) for i in range(count)]
    across = []
    for i in range(1, count, 2):
        if periodic or i + 1 < count:
            across += [(i, (i + 1) % count), ((i + 1) % count, i)]
    return near, across


def swap_sides(near, across, axis, periodic):
    near_pairs, across_pairs = pairs_of(axis, periodic)
    return lax.ppermute(near, axis, near_pairs), lax.ppermute(across, axis, across_pairs)


def near_side(low, high, axis="lat"):
    odd = (lax.axis_index(axis) & 1) == 1
    return jnp.where(odd, low, high), jnp.where(odd, high, low)


def pack_kernel(
    n, cap, stations, count_ref, band_ref, station_ref, var_ref, dep_ref, coef_ref, *rest
):
    half = n // 2
    own, swap = rest[:2]
    through = rest[2 : half + 1]
    near, across = rest[half + 1 : half + 3]
    (dep, band, station, var, edge, buf, pos_v, pos_s, sem) = rest[half + 3 :]
    me = lax.axis_index("lat")
    rows, lanes = band.shape
    lat_cells = coef_ref.shape[2]
    loads = [
        pltpu.make_async_copy(src, dst, sem.at[k])
        for k, (src, dst) in enumerate(
            (
                (band_ref, band),
                (station_ref, station),
                (var_ref, var),
                (dep_ref, dep),
                (coef_ref.at[:, :, pl.ds(0, 8)], edge.at[0]),
                (coef_ref.at[:, :, pl.ds(lat_cells - 8, 8)], edge.at[1]),
            )
        )
    ]
    start_all(loads)
    wait_all(loads[:3])
    count = count_ref[0, 0]
    slot = (
        lax.broadcasted_iota(jnp.int32, (rows, lanes), 0) * lanes
        + lax.broadcasted_iota(jnp.int32, (rows, lanes), 1)
    )
    far = (band[...] >> 1) - (me >> 1)
    far = jnp.where(far < 0, far + half, far)
    group = jnp.where((band[...] & 1) == (me & 1), far, far + half)
    group = jnp.where(slot < count, group, n)
    masks = jnp.concatenate([(group == s).astype(jnp.float32) for s in range(n)], axis=0)
    before = lax.broadcasted_iota(jnp.int32, (lanes, lanes), 0) < lax.broadcasted_iota(
        jnp.int32, (lanes, lanes), 1
    )
    prefix = jnp.dot(masks, before.astype(jnp.float32), preferred_element_type=jnp.float32)
    totals = jnp.dot(
        masks, jnp.ones((lanes, lanes), jnp.float32), preferred_element_type=jnp.float32
    )
    a = lax.broadcasted_iota(jnp.int32, (rows * n, rows * n), 0)
    b = lax.broadcasted_iota(jnp.int32, (rows * n, rows * n), 1)
    earlier = ((a // rows == b // rows) & (b < a)).astype(jnp.float32)
    offset = jnp.dot(earlier, totals, preferred_element_type=jnp.float32)
    ranks = (prefix + offset).astype(jnp.int32)
    rank = jnp.zeros((rows, lanes), jnp.int32)
    for s in range(n):
        rank = jnp.where(group == s, ranks[s * rows : (s + 1) * rows], rank)
    pos_v[...] = group * STRIDE + rank
    place_map = pltpu.make_async_copy(pos_v, pos_s, sem.at[0])
    place_map.start()
    code = var[...] * stations + station[...]
    upper = (code >> 6).astype(jnp.float32)
    lower = (code & 63).astype(jnp.float32)
    width = -(-cap // lanes) * lanes
    which = lax.broadcasted_iota(jnp.int32, (n, lanes), 0)
    order = lax.broadcasted_iota(jnp.int32, (width, lanes), 0)
    codes = jnp.zeros((2 * n, width), jnp.float32)
    for k in range(rows):
        mine = which == group[k : k + 1]
        parts = jnp.concatenate(
            [jnp.where(mine, upper[k : k + 1], 0.0), jnp.where(mine, lower[k : k + 1], 0.0)], 0
        )
        codes += lax.dot_general(
            parts,
            (order == rank[k : k + 1]).astype(jnp.float32),
            (((1,), (1,)), ((), ())),
            preferred_element_type=jnp.float32,
        )
    codes = codes[:n] * 64.0 + codes[n:]
    counts = offset + totals
    size = cap + HEADER

    def target(s):
        if s == 0:
            return own, 0
        if s < half:
            return through[s - 1], 0
        return swap, (s - half) * size

    for s in range(n):
        to, at = target(s)
        for j in range(width // lanes):
            to[pl.ds(at + cap + j, 1), :] = codes[s : s + 1, j * lanes : (j + 1) * lanes]
        to[pl.ds(at + cap + HEADER - 1, 1), :] = counts[(s + 1) * rows - 1 : (s + 1) * rows]
    wait_all(loads[3:])
    fields, lons = edge.shape[1:3]
    odd = me & 1

    def strip(i, carry):
        for f in range(fields):
            near[pl.ds((f * lons + i) * 2, 2), :] = edge[1 - odd, f, i, pl.ds(6 - 6 * odd, 2), :]
            across[pl.ds((f * lons + i) * 2, 2), :] = edge[odd, f, i, pl.ds(6 * odd, 2), :]
        return carry

    lax.fori_loop(0, lons, strip, 0)
    place_map.wait()

    def place(g, carry):
        base = pl.multiple_of(g * 16, 16)
        row, col = base >> 7, base & 127
        for k in range(16):
            buf[pl.ds(pos_s[row, col + k], 1), :] = dep[pl.ds(base + k, 1), :]
        return carry

    lax.fori_loop(0, (count + 15) >> 4, place, 0)
    for s in range(n):
        to, at = target(s)
        to[pl.ds(at, cap), :] = buf[pl.ds(s * STRIDE, cap), :]


def pack(n, cap, stations, count, band, station, var, dep, coef):
    rows = dep.shape[0] // LANES
    fields, lons = coef.shape[:2]
    size, half = cap + HEADER, n // 2
    strip = (fields * lons * 2, LANES)
    shapes = [(size, LANES), (half * size, LANES)]
    shapes += [
        (size if s == half // 2 else 2 * size, LANES) for s in range(1, half)
    ] + [strip, strip]
    hbm = pl.BlockSpec(memory_space=pltpu.HBM)
    vm = pl.BlockSpec(memory_space=V)
    return pl.pallas_call(
        functools.partial(pack_kernel, n, cap, stations),
        out_shape=tuple(V(shape, jnp.float32) for shape in shapes),
        in_specs=[pl.BlockSpec(memory_space=pltpu.SMEM)] + [hbm] * 5,
        out_specs=(vm,) * len(shapes),
        scratch_shapes=[
            V(dep.shape, jnp.float32),
            V((rows, LANES), jnp.int32),
            V((rows, LANES), jnp.int32),
            V((rows, LANES), jnp.int32),
            V((2, fields, lons, 8, LANES), jnp.float32),
            V((n * STRIDE + HEADER + STRIDE, LANES), jnp.float32),
            V((rows, LANES), jnp.int32),
            pltpu.SMEM((rows, LANES), jnp.int32),
            pltpu.SemaphoreType.DMA((6,)),
        ],
        compiler_params=params(),
        name="pack",
    )(count, *(in_hbm(array) for array in (band, station, var, dep, coef)))


def relay_kernel(shifts, size, swapped, *rest):
    for s, to in zip(shifts, rest[len(rest) - len(shifts) :]):
        to[pl.ds(size, size), :] = swapped[pl.ds(s * size, size), :]


def relay(swapped, through, shifts, size, after=()):
    k = len(shifts)
    vm = pl.BlockSpec(memory_space=V)
    picked = [through[s - 1] for s in shifts]
    return pl.pallas_call(
        functools.partial(relay_kernel, shifts, size),
        out_shape=tuple(V(array.shape, jnp.float32) for array in picked),
        in_specs=[vm] * (k + 1 + len(after)),
        out_specs=(vm,) * k,
        input_output_aliases={j + 1: j for j in range(k)},
        compiler_params=params(),
        name="relay",
    )(in_vmem(swapped), *(in_vmem(array) for array in (*picked, *after)))


def alone_kernel(start, swapped, *rest):
    to = rest[-1]
    to[...] = swapped[pl.ds(start, to.shape[0]), :]


def alone(swapped, s, size, after=()):
    vm = pl.BlockSpec(memory_space=V)
    return pl.pallas_call(
        functools.partial(alone_kernel, s * size),
        out_shape=V((size, LANES), jnp.float32),
        in_specs=[vm] * (1 + len(after)),
        out_specs=vm,
        compiler_params=params(),
        name="alone",
    )(in_vmem(swapped), *(in_vmem(array) for array in after))


def open_header(packet, base, cap, view, header, sem):
    view[...] = packet[pl.ds(base + cap, HEADER), :].astype(jnp.int32)
    copy = pltpu.make_async_copy(view, header, sem)
    copy.start()
    return copy


def scatter_packet(table_ref, packet, start, header, state):
    unroll = 8
    count = header[HEADER - 1, 0]

    def some(g, carry):
        base = g * unroll
        major, minor = base >> 7, base & 127
        rows = [table_ref[0, header[major, minor + k]] for k in range(unroll)]
        for k in range(unroll):
            state[pl.ds(rows[k], 1), :] += packet[pl.ds(start + base + k, 1), :]
        return carry

    def one(j, carry):
        row = table_ref[0, header[j >> 7, j & 127]]
        state[pl.ds(row, 1), :] += packet[pl.ds(start + j, 1), :]
        return carry

    whole = count >> 3
    lax.fori_loop(0, whole, some, 0)
    lax.fori_loop(whole * unroll, count, one, 0)


def first_kernel(
    k, lons, lats, cap, table_ref, adjoint_ref, *rest
):
    packets, (state, full) = rest[:k], rest[len(rest) - 2 * k - 3 : len(rest) - 2 * k - 1]
    rest = rest[len(rest) - 2 * k - 1 :]
    views, headers, sem = rest[:k], rest[k : 2 * k], rest[2 * k]
    span = lats + 4
    ring = (lons + 4) * span
    nv = state.shape[0] // ring
    load = pltpu.make_async_copy(adjoint_ref, full, sem.at[0])
    load.start()
    opened = [
        open_header(packets[j], 0, cap, views[j], headers[j], sem.at[j + 1]) for j in range(k)
    ]
    load.wait()

    def fill(i, carry):
        for v in range(nv):
            to = v * ring + (i + 2) * span + 2
            at = (v * lons + i) * lats
            for r in range(0, lats, 8):
                state[pl.ds(to + r, 8), :] = full[pl.ds(pl.multiple_of(at + r, 8), 8), :]
        return carry

    lax.fori_loop(0, lons, fill, 0)
    wait_all(opened)
    for j in range(k):
        scatter_packet(table_ref, packets[j], 0, headers[j], state)


def scatter_first(table, adjoint, packets, cap, shape, after=()):
    nv, lons, lats = shape
    k = len(packets)
    hbm = pl.BlockSpec(memory_space=pltpu.HBM)
    ring = (lons + 4) * (lats + 4)
    return pl.pallas_call(
        functools.partial(first_kernel, k, lons, lats, cap),
        out_shape=V((nv * ring, LANES), jnp.float32),
        in_specs=[pl.BlockSpec(memory_space=pltpu.SMEM), hbm]
        + [pl.BlockSpec(memory_space=V)] * (k + len(after)),
        out_specs=pl.BlockSpec(memory_space=V),
        scratch_shapes=[
            V(adjoint.shape, jnp.float32),
            *[V((HEADER, LANES), jnp.int32)] * k,
            *[pltpu.SMEM((HEADER, LANES), jnp.int32)] * k,
            pltpu.SemaphoreType.DMA((k + 1,)),
        ],
        compiler_params=params(),
        name="scatter_own",
    )(table, in_hbm(adjoint), *(in_vmem(array) for array in (*packets, *after)))


def more_kernel(k, lons, lats, cap, last, table_ref, *rest):
    size = cap + HEADER
    packets = [(rest[j], base) for j in range(k) for base in range(0, rest[j].shape[0], size)]
    m = len(packets)
    rest = rest[len(rest) - (3 if last else 1) - 2 * m - 1 :]
    outs, rest = rest[: 3 if last else 1], rest[3 if last else 1 :]
    views, headers, sem = rest[:m], rest[m : 2 * m], rest[2 * m]
    state = outs[0]
    opened = [
        open_header(*packets[j], cap, views[j], headers[j], sem.at[j]) for j in range(m)
    ]
    wait_all(opened)
    for j in range(m):
        scatter_packet(table_ref, *packets[j], headers[j], state)
    if not last:
        return
    near, across = outs[1:]
    span = lats + 4
    ring = (lons + 4) * span
    nv = state.shape[0] // ring
    near_row, across_row = near_side(2, lats)

    def strip(i, carry):
        for v in range(nv):
            at = v * ring + (i + 2) * span
            to = (v * lons + i) * 2
            near[pl.ds(to, 2), :] = state[pl.ds(at + near_row, 2), :]
            across[pl.ds(to, 2), :] = state[pl.ds(at + across_row, 2), :]
        return carry

    lax.fori_loop(0, lons, strip, 0)


def scatter_more(table, state, packets, cap, shape, last, after=()):
    nv, lons, lats = shape
    k = len(packets)
    m = sum(packet.shape[0] // (cap + HEADER) for packet in packets)
    vm = pl.BlockSpec(memory_space=V)
    out = V(state.shape, jnp.float32)
    strip = V((nv * lons * 2, LANES), jnp.float32)
    return pl.pallas_call(
        functools.partial(more_kernel, k, lons, lats, cap, last),
        out_shape=(out, strip, strip) if last else out,
        in_specs=[pl.BlockSpec(memory_space=pltpu.SMEM)] + [vm] * (k + 1 + len(after)),
        out_specs=(vm, vm, vm) if last else vm,
        input_output_aliases={k + 1: 0},
        scratch_shapes=[V((HEADER, LANES), jnp.int32)] * m
        + [pltpu.SMEM((HEADER, LANES), jnp.int32)] * m
        + [pltpu.SemaphoreType.DMA((m,))],
        compiler_params=params(),
        name="scatter_last" if last else "scatter_more",
    )(
        table,
        *(in_vmem(packet) for packet in packets),
        in_vmem(state),
        *(in_vmem(array) for array in after),
    )


def widen_kernel(coef_ref, near_ref, across_ref, after, ring_out, near_lon, across_lon, own, sem):
    fields, lons, lats, _ = coef_ref.shape
    span = lats + 4
    ring = (lons + 4) * span
    near_row, across_row = near_side(0, lats + 2)
    near_at, across_at = near_side(2 * span, lons * span, "lon")
    run([pltpu.make_async_copy(coef_ref, own, sem)])

    def fill(i, carry):
        for f in range(fields):
            to = f * ring + (i + 2) * span
            at = (f * lons + i) * 2
            for r in range(0, lats, 8):
                ring_out[pl.ds(to + 2 + r, 8), :] = own[f, i, r : r + 8]
            ring_out[pl.ds(to + near_row, 2), :] = near_ref[pl.ds(at, 2), :]
            ring_out[pl.ds(to + across_row, 2), :] = across_ref[pl.ds(at, 2), :]
        return carry

    lax.fori_loop(0, lons, fill, 0)
    take_lons(ring_out, near_lon, across_lon, fields, ring, 2 * span, near_at, across_at)


def take_lons(ring_ref, near, across, count, ring, size, near_at, across_at):
    for f in range(count):
        near[pl.ds(f * size, size), :] = ring_ref[pl.ds(f * ring + near_at, size), :]
        across[pl.ds(f * size, size), :] = ring_ref[pl.ds(f * ring + across_at, size), :]


def put_lons(ring_ref, near, across, count, ring, size, near_at, across_at):
    for f in range(count):
        ring_ref[pl.ds(f * ring + near_at, size), :] = near[pl.ds(f * size, size), :]
        ring_ref[pl.ds(f * ring + across_at, size), :] = across[pl.ds(f * size, size), :]


def widen(coef, near, across, after):
    fields, lons, lats, _ = coef.shape
    span = lats + 4
    vm = pl.BlockSpec(memory_space=V)
    edge = V((fields * 2 * span, LANES), jnp.float32)
    return pl.pallas_call(
        widen_kernel,
        out_shape=(V((fields * (lons + 4) * span, LANES), jnp.float32), edge, edge),
        in_specs=[pl.BlockSpec(memory_space=pltpu.HBM), vm, vm, vm],
        out_specs=(vm, vm, vm),
        scratch_shapes=[V(coef.shape, jnp.float32), pltpu.SemaphoreType.DMA],
        compiler_params=params(),
        name="widen",
    )(in_hbm(coef), in_vmem(near), in_vmem(across), in_vmem(after))


def combine_kernel(lons, lats, ring_ref, near, across, out_ref, field):
    me = lax.axis_index("lat")
    total = lats * lax.axis_size("lat")
    span, rim = lats + 4, lats + 2
    ring = (lons + 4) * span
    size = rim_rows(lons, lats)
    field[...] = ring_ref[...]
    ends = near_side(0, (lons + 2) * span, "lon")
    put_lons(field, near, across, field.shape[0] // ring, ring, 2 * span, *ends)
    lev = lax.broadcasted_iota(jnp.int32, (8, LANES), 1)
    row = lax.broadcasted_iota(jnp.int32, (8, LANES), 0)

    def one(i, carry):
        for r in chunks(rim):
            lat = row + (r - 1) + me * lats
            inside = (lat >= 0) & (lat < total)
            at = (i + 1) * span + r + 1

            def wind(f, shift, at=at):
                return ADVECT_SCALE * field[pl.ds(f * ring + at + shift, 8), :]

            def half(shift, at=at):
                return 0.5 * field[pl.ds(2 * ring + at + shift, 8), :]

            mine = half(0)
            east_factor = wind(0, 0) + (mine + half(span))
            west_factor = (mine + half(-span)) - wind(0, -span)
            north_factor = wind(1, 0) + (mine + half(1))
            south_factor = (mine + half(-1)) - wind(1, -1)
            up = jnp.where(lev < LANES - 1, mine + pltpu.roll(mine, LANES - 1, 1), 0.0)
            down = jnp.where(lev > 0, mine + pltpu.roll(mine, 1, 1), 0.0)
            centre = 1.0 - (
                ((east_factor + west_factor) + (north_factor + south_factor)) + (up + down)
            )
            factors = (centre, east_factor, west_factor, north_factor, south_factor, up, down)
            for k, value in enumerate(factors):
                out_ref[pl.ds(k * size + i * rim + r, 8), :] = jnp.where(inside, value, 0.0)
        return carry

    lax.fori_loop(0, lons + 2, one, 0)


def combine(ring, near, across, lons, lats):
    vm = pl.BlockSpec(memory_space=V)
    return pl.pallas_call(
        functools.partial(combine_kernel, lons, lats),
        out_shape=V((7 * rim_rows(lons, lats), LANES), jnp.float32),
        in_specs=[vm, vm, vm],
        out_specs=vm,
        scratch_shapes=[V(ring.shape, jnp.float32)],
        compiler_params=params(),
        name="combine",
    )(in_vmem(ring), in_vmem(near), in_vmem(across))


def rim_rows(lons, lats):
    return -(-(lons + 2) * (lats + 2) // 8) * 8


def chunks(rows):
    starts = list(range(0, rows - 7, 8))
    if starts[-1] + 8 < rows:
        starts.append(rows - 8)
    return starts


def shift_matrix():
    k = lax.broadcasted_iota(jnp.int32, (2 * LANES, 2 * LANES), 0) & (LANES - 1)
    j = lax.broadcasted_iota(jnp.int32, (2 * LANES, 2 * LANES), 1)
    take = ((j < LANES) & (k == j + 1)) | ((j >= LANES) & (k == j - LANES - 1))
    return take.astype(jnp.float32).astype(jnp.bfloat16)


def shifted(centres, matrix):
    block = jnp.concatenate(centres, axis=0)
    high = block.astype(jnp.bfloat16)
    low = (block - high.astype(jnp.float32)).astype(jnp.bfloat16)
    both = jnp.dot(
        jnp.concatenate([high, low], axis=1), matrix, preferred_element_type=jnp.float32
    )
    return [
        (both[8 * k : 8 * k + 8, :LANES], both[8 * k : 8 * k + 8, LANES:])
        for k in range(len(centres))
    ]


def rolled(centre):
    return pltpu.roll(centre, LANES - 1, 1), pltpu.roll(centre, 1, 1)


def weighted(factors, source, at, east, rows=None, levels=None):
    rows = rows or (lambda start: pl.ds(start, 8))
    centre = source[rows(at), :]
    above, below = levels or rolled(centre)
    total = factors[0] * centre + factors[1] * source[rows(at + east), :]
    other = factors[2] * source[rows(at - east), :] + factors[3] * source[rows(at + 1), :]
    third = factors[4] * source[rows(at - 1), :] + factors[5] * above
    return (total + other) + (third + factors[6] * below)


def step_rows(coef_ref, source, nv, spots, stride, east, put, matrix):
    size = coef_ref.shape[0] // 7
    levels = [None] * (len(spots) * nv)
    if matrix is not None:
        part = int(len(levels) * 0.5) // 2 * 2
        levels[:part] = shifted(
            [source[pl.ds(v * stride + at, 8), :] for _, at in spots for v in range(nv)][:part],
            matrix,
        )
    for k, (row, at) in enumerate(spots):
        factors = [coef_ref[pl.ds(f * size + row, 8), :] for f in range(7)]
        for v in range(nv):
            put(
                k,
                v,
                weighted(
                    factors, source, v * stride + at, east, levels=levels[k * nv + v]
                ),
            )


def first_step(coef_ref, state, mid, nv, lons, lats, places, starts, matrix=None):
    span, rim = lats + 4, lats + 2
    ring, size = (lons + 4) * span, rim_rows(lons, lats)
    spots = [(i * rim + r, (i + 1) * span + r + 1) for i in places for r in starts]

    def put(k, v, value):
        mid[pl.ds(v * size + spots[k][0], 8), :] = value

    step_rows(coef_ref, state, nv, spots, ring, span, put, matrix)


def first_step_along(coef_ref, state, mid, nv, lons, lats, i, r):
    span, rim = lats + 4, lats + 2
    ring, size = (lons + 4) * span, rim_rows(lons, lats)

    def rim_at(start):
        return pl.ds(start, 8, stride=rim)

    def ring_at(start):
        return pl.ds(start, 8, stride=span)

    factors = [coef_ref[rim_at(k * size + i * rim + r), :] for k in range(7)]
    for v in range(nv):
        mid[rim_at(v * size + i * rim + r), :] = weighted(
            factors, state, v * ring + (i + 1) * span + r + 1, span, ring_at
        )


def second_step(coef_ref, mid, out, nv, lons, lats, places, place, matrix=None):
    rim = lats + 2
    spots = [
        ((i + 1) * rim + r + 1, (i + 1) * rim + r + 1) for i in places for r in range(0, lats, 8)
    ]
    each = lats // 8

    def put(k, v, value):
        at = place(v, k // each) + (k % each) * 8
        out[pl.ds(pl.multiple_of(at, 8), 8), :] = value

    step_rows(coef_ref, mid, nv, spots, rim_rows(lons, lats), rim, put, matrix)


def insert_kernel(lons, lats, state_in, near, across, state, near_lon, across_lon):
    span = lats + 4
    ring = (lons + 4) * span
    nv = state.shape[0] // ring

    near_row, across_row = near_side(0, lats + 2)

    def strip(i, carry):
        for v in range(nv):
            at = v * ring + (i + 2) * span
            frm = (v * lons + i) * 2
            state[pl.ds(at + near_row, 2), :] = near[pl.ds(frm, 2), :]
            state[pl.ds(at + across_row, 2), :] = across[pl.ds(frm, 2), :]
        return carry

    lax.fori_loop(0, lons, strip, 0)
    ends = near_side(2 * span, lons * span, "lon")
    take_lons(state, near_lon, across_lon, nv, ring, 2 * span, *ends)


def insert(state, near, across, shape):
    nv, lons, lats = shape
    vm = pl.BlockSpec(memory_space=V)
    edge = V((nv * 2 * (lats + 4), LANES), jnp.float32)
    return pl.pallas_call(
        functools.partial(insert_kernel, lons, lats),
        out_shape=(V(state.shape, jnp.float32), edge, edge),
        in_specs=[vm] * 3,
        out_specs=(vm,) * 3,
        input_output_aliases={0: 0},
        compiler_params=params(),
        name="insert",
    )(in_vmem(state), in_vmem(near), in_vmem(across))


def early_kernel(nv, lons, lats, coef_ref, state, mid):
    starts = [r + 2 for r in chunks(lats - 2)]
    matrix = shift_matrix()

    def first(i, carry):
        at = jnp.minimum(2 + GROUP * i, lons - GROUP)
        places = [at + k for k in range(GROUP)]
        first_step(coef_ref, state, mid, nv, lons, lats, places, starts, matrix)
        return carry

    lax.fori_loop(0, -(-(lons - 2) // GROUP), first, 0)


def early(coef, state, shape):
    nv, lons, lats = shape
    vm = pl.BlockSpec(memory_space=V)
    return pl.pallas_call(
        functools.partial(early_kernel, nv, lons, lats),
        out_shape=V((nv * rim_rows(lons, lats), LANES), jnp.float32),
        in_specs=[vm, vm],
        out_specs=vm,
        compiler_params=params(),
        name="early",
    )(in_vmem(coef), in_vmem(state))


def inner_kernel(lons, lats, coef_ref, state, mid_in, mid, out_ref, out, sem):
    nv = out.shape[0] // (lons * lats)
    cells = lons * lats
    for r in (0, 1, lats, lats + 1):

        def first(k, carry, r=r):
            i = jnp.minimum(2 + 8 * k, lons - 8)
            first_step_along(coef_ref, state, mid, nv, lons, lats, i, r)
            return carry

        lax.fori_loop(0, -(-(lons - 2) // 8), first, 0)

    matrix = shift_matrix()

    def second(i, carry):
        second_step(
            coef_ref,
            mid,
            out,
            nv,
            lons,
            lats,
            [2 + GROUP * i + k for k in range(GROUP)],
            lambda v, k: v * cells + (2 + GROUP * i + k) * lats,
            matrix,
        )
        return carry

    parts = 4
    groups = (lons - 4) // GROUP
    ends = [0] + [groups * p // parts for p in range(1, parts)] + [groups]
    edges = [2 + GROUP * g for g in ends]
    copies = []
    for p in range(parts):
        lax.fori_loop(ends[p], ends[p + 1], second, 0)
        for v in range(nv):
            span = pl.ds(v * cells + edges[p] * lats, (edges[p + 1] - edges[p]) * lats)
            copy = pltpu.make_async_copy(out.at[span], out_ref.at[span], sem.at[p * nv + v])
            copy.start()
            copies.append(copy)
    wait_all(copies)


def inner(coef, state, mid, shape):
    nv, lons, lats = shape
    vm = pl.BlockSpec(memory_space=V)
    return pl.pallas_call(
        functools.partial(inner_kernel, lons, lats),
        out_shape=(
            V(mid.shape, jnp.float32),
            jax.ShapeDtypeStruct((nv * lons * lats, LANES), jnp.float32),
        ),
        in_specs=[vm, vm, vm],
        out_specs=(vm, pl.BlockSpec(memory_space=pltpu.HBM)),
        input_output_aliases={2: 0},
        scratch_shapes=[
            V((nv * lons * lats, LANES), jnp.float32),
            pltpu.SemaphoreType.DMA((4 * nv,)),
        ],
        compiler_params=params(),
        name="inner",
    )(in_vmem(coef), in_vmem(state), in_vmem(mid))


def outer_kernel(
    lons, lats, coef_ref, state_in, mid_in, near, across, out_in, state, mid, out_ref, out, sem
):
    span = lats + 4
    ring = (lons + 4) * span
    nv = state.shape[0] // ring
    cells = lons * lats
    ends = near_side(0, (lons + 2) * span, "lon")
    put_lons(state, near, across, nv, ring, 2 * span, *ends)

    def first(k, carry):
        i = jnp.where(k < 2, k, lons - 2 + k)
        first_step(coef_ref, state, mid, nv, lons, lats, (i,), chunks(lats + 2))
        return carry

    lax.fori_loop(0, 4, first, 0)

    def second(k, carry):
        i = jnp.where(k < 2, k, lons - 4 + k)
        second_step(
            coef_ref, mid, out, nv, lons, lats, (i,), lambda v, _: (v * 4 + k) * lats
        )
        return carry

    lax.fori_loop(0, 4, second, 0)
    copies = []
    for v in range(nv):
        for side, at in ((0, 0), (1, lons - 2)):
            copies.append(
                pltpu.make_async_copy(
                    out.at[pl.ds((v * 4 + 2 * side) * lats, 2 * lats)],
                    out_ref.at[pl.ds(v * cells + at * lats, 2 * lats)],
                    sem.at[v * 2 + side],
                )
            )
    run(copies)


def outer(coef, state, mid, near, across, out, shape):
    nv, lons, lats = shape
    vm = pl.BlockSpec(memory_space=V)
    hbm = pl.BlockSpec(memory_space=pltpu.HBM)
    return pl.pallas_call(
        functools.partial(outer_kernel, lons, lats),
        out_shape=(
            V(state.shape, jnp.float32),
            V(mid.shape, jnp.float32),
            jax.ShapeDtypeStruct(out.shape, jnp.float32),
        ),
        in_specs=[vm] * 5 + [hbm],
        out_specs=(vm, vm, hbm),
        input_output_aliases={1: 0, 2: 1, 5: 2},
        scratch_shapes=[V((nv * 4 * lats, LANES), jnp.float32), pltpu.SemaphoreType.DMA((2 * nv,))],
        compiler_params=params(),
        name="outer",
    )(in_vmem(coef), in_vmem(state), in_vmem(mid), in_vmem(near), in_vmem(across), out)[2]


def body(
    adjoint_in, departures, obs_band, obs_station, obs_var, counts, station_cell, coefficients
):
    nv, lons, lats, levels = adjoint_in.shape
    shape = (nv, lons, lats)
    slots = departures.shape[2]
    n = lax.axis_size("lat")
    cap = -(-3 * slots // n // 8) * 8
    stations = station_cell.shape[2]
    square = (slots // LANES, LANES)
    own, swap, *rest = pack(
        n,
        cap,
        stations,
        counts,
        obs_band.reshape(square),
        obs_station.reshape(square),
        obs_var.reshape(square),
        departures.reshape(slots, levels),
        coefficients,
    )
    through, (near, across) = rest[:-2], rest[-2:]
    swapped = lax.ppermute(swap, "lat", [(i, i ^ 1) for i in range(n)])
    near, across = swap_sides(near, across, "lat", False)
    size = cap + HEADER
    order = sorted(range(1, n // 2), key=lambda s: abs(4 * s - n))
    cell = station_cell.reshape(1, stations)
    span = lats + 4
    spot = (cell // lats + 2) * span + cell % lats + 2
    tile = (lons + 4) * span
    table = jnp.concatenate([spot + v * tile for v in range(nv)], axis=1)
    def send(s, packet):
        return lax.ppermute(packet, "lat", [(i, (i + 2 * s) % n) for i in range(n)])

    def send_pairs(shifts, after):
        return [
            send(s, packet)
            for s, packet in zip(shifts, relay(swapped, through, shifts, size, after))
        ]

    middle = 1 + (len(order) - 1) // 2
    adjoint = adjoint_in.reshape(nv * lons * lats, levels)
    ahead = send(order[0], through[order[0] - 1])
    second = send_pairs(order[1:middle], ())
    ring, near, across = widen(coefficients, near, across, swapped)
    third = send_pairs(order[middle:], (ring,))
    near, across = swap_sides(near, across, "lon", True)
    coef = combine(ring, near, across, lons, lats)
    state = scatter_first(table, adjoint, [own, swapped, ahead], cap, shape, (coef,))
    moved = [send(order[0], alone(swapped, order[0], size, (state,)))]
    state = scatter_more(table, state, second, cap, shape, False)
    state = scatter_more(table, state, third, cap, shape, False)
    state, near, across = scatter_more(table, state, moved, cap, shape, True)
    near, across = swap_sides(near, across, "lat", False)
    mid = early(coef, state, shape)
    state, near, across = insert(state, near, across, shape)
    near, across = swap_sides(near, across, "lon", True)
    mid, out = inner(coef, state, mid, shape)
    out = outer(coef, state, mid, near, across, out, shape)
    return out.reshape(adjoint_in.shape)


def solution(mesh):
    in_specs = (
        P(None, "lon", "lat", None),
        P("lon", "lat", None, None),
        P("lon", "lat", None, None),
        P("lon", "lat", None),
        P("lon", "lat", None),
        P("lon", "lat"),
        P("lon", "lat", None),
        P(None, "lon", "lat", None),
    )
    out_specs = P(None, "lon", "lat", None)
    return jax.shard_map(body, mesh=mesh, in_specs=in_specs, out_specs=out_specs, check_vma=False)
```

```python
import functools

import jax
import jax.numpy as jnp
from jax import lax
from jax.experimental import pallas as pl
from jax.experimental.pallas import tpu as pltpu
from jax.sharding import PartitionSpec as P

ADVECT_SCALE = 0.2
LANES = 128
GROUP = 4
STRIDE = 1024
HEADER = 8
VMEM_LIMIT = 40 * 1024 * 1024
V = pltpu.VMEM


def in_vmem(array):
    return pltpu.with_memory_space_constraint(array, V)


def in_hbm(array):
    return pltpu.with_memory_space_constraint(array, pltpu.HBM)


def params():
    return pltpu.CompilerParams(vmem_limit_bytes=VMEM_LIMIT)


def start_all(copies):
    for copy in copies:
        copy.start()


def wait_all(copies):
    for copy in copies:
        copy.wait()


def run(copies):
    start_all(copies)
    wait_all(copies)


def pairs_of(axis, periodic):
    count = lax.axis_size(axis)
    near = [(i, i ^ 1) for i in range(count)]
    across = []
    for i in range(1, count, 2):
        if periodic or i + 1 < count:
            across += [(i, (i + 1) % count), ((i + 1) % count, i)]
    return near, across


def swap_sides(near, across, axis, periodic):
    near_pairs, across_pairs = pairs_of(axis, periodic)
    return lax.ppermute(near, axis, near_pairs), lax.ppermute(across, axis, across_pairs)


def near_side(low, high, axis="lat"):
    odd = (lax.axis_index(axis) & 1) == 1
    return jnp.where(odd, low, high), jnp.where(odd, high, low)


def pack_kernel(
    n, cap, stations, count_ref, band_ref, station_ref, var_ref, dep_ref, coef_ref, *rest
):
    half = n // 2
    own, swap = rest[:2]
    through = rest[2 : half + 1]
    across = rest[half + 1]
    (dep, band, station, var, edge, buf, pos_v, pos_s, sem) = rest[half + 2 :]
    me = lax.axis_index("lat")
    rows, lanes = band.shape
    lat_cells = coef_ref.shape[2]
    loads = [
        pltpu.make_async_copy(src, dst, sem.at[k])
        for k, (src, dst) in enumerate(
            (
                (band_ref, band),
                (station_ref, station),
                (var_ref, var),
                (dep_ref, dep),
                (coef_ref.at[:, :, pl.ds(0, 8)], edge.at[0]),
                (coef_ref.at[:, :, pl.ds(lat_cells - 8, 8)], edge.at[1]),
            )
        )
    ]
    start_all(loads)
    wait_all(loads[:3])
    count = count_ref[0, 0]
    slot = (
        lax.broadcasted_iota(jnp.int32, (rows, lanes), 0) * lanes
        + lax.broadcasted_iota(jnp.int32, (rows, lanes), 1)
    )
    far = (band[...] >> 1) - (me >> 1)
    far = jnp.where(far < 0, far + half, far)
    group = jnp.where((band[...] & 1) == (me & 1), far, far + half)
    group = jnp.where(slot < count, group, n)
    masks = jnp.concatenate([(group == s).astype(jnp.float32) for s in range(n)], axis=0)
    before = lax.broadcasted_iota(jnp.int32, (lanes, lanes), 0) < lax.broadcasted_iota(
        jnp.int32, (lanes, lanes), 1
    )
    prefix = jnp.dot(masks, before.astype(jnp.float32), preferred_element_type=jnp.float32)
    totals = jnp.dot(
        masks, jnp.ones((lanes, lanes), jnp.float32), preferred_element_type=jnp.float32
    )
    a = lax.broadcasted_iota(jnp.int32, (rows * n, rows * n), 0)
    b = lax.broadcasted_iota(jnp.int32, (rows * n, rows * n), 1)
    earlier = ((a // rows == b // rows) & (b < a)).astype(jnp.float32)
    offset = jnp.dot(earlier, totals, preferred_element_type=jnp.float32)
    ranks = (prefix + offset).astype(jnp.int32)
    rank = jnp.zeros((rows, lanes), jnp.int32)
    for s in range(n):
        rank = jnp.where(group == s, ranks[s * rows : (s + 1) * rows], rank)
    pos_v[...] = group * STRIDE + rank
    place_map = pltpu.make_async_copy(pos_v, pos_s, sem.at[0])
    place_map.start()
    code = var[...] * stations + station[...]
    upper = (code >> 6).astype(jnp.float32)
    lower = (code & 63).astype(jnp.float32)
    width = -(-cap // lanes) * lanes
    which = lax.broadcasted_iota(jnp.int32, (n, lanes), 0)
    order = lax.broadcasted_iota(jnp.int32, (width, lanes), 0)
    codes = jnp.zeros((2 * n, width), jnp.float32)
    for k in range(rows):
        mine = which == group[k : k + 1]
        parts = jnp.concatenate(
            [jnp.where(mine, upper[k : k + 1], 0.0), jnp.where(mine, lower[k : k + 1], 0.0)], 0
        )
        codes += lax.dot_general(
            parts,
            (order == rank[k : k + 1]).astype(jnp.float32),
            (((1,), (1,)), ((), ())),
            preferred_element_type=jnp.float32,
        )
    codes = codes[:n] * 64.0 + codes[n:]
    counts = offset + totals
    size = cap + HEADER

    def target(s):
        if s == 0:
            return own, 0
        if s < half:
            return through[s - 1], 0
        return swap, (s - half) * size

    for s in range(n):
        to, at = target(s)
        for j in range(width // lanes):
            to[pl.ds(at + cap + j, 1), :] = codes[s : s + 1, j * lanes : (j + 1) * lanes]
        to[pl.ds(at + cap + HEADER - 1, 1), :] = counts[(s + 1) * rows - 1 : (s + 1) * rows]
    wait_all(loads[3:])
    fields, lons = edge.shape[1:3]
    odd = me & 1

    def strip(i, carry):
        for f in range(fields):
            row = (f * lons + i) * 2
            swap[pl.ds(half * size + row, 2), :] = edge[1 - odd, f, i, pl.ds(6 - 6 * odd, 2), :]
            across[pl.ds(row, 2), :] = edge[odd, f, i, pl.ds(6 * odd, 2), :]
        return carry

    lax.fori_loop(0, lons, strip, 0)
    place_map.wait()

    def place(g, carry):
        base = pl.multiple_of(g * 16, 16)
        row, col = base >> 7, base & 127
        for k in range(16):
            buf[pl.ds(pos_s[row, col + k], 1), :] = dep[pl.ds(base + k, 1), :]
        return carry

    lax.fori_loop(0, (count + 15) >> 4, place, 0)
    for s in range(n):
        to, at = target(s)
        to[pl.ds(at, cap), :] = buf[pl.ds(s * STRIDE, cap), :]


def pack(n, cap, stations, count, band, station, var, dep, coef):
    rows = dep.shape[0] // LANES
    fields, lons = coef.shape[:2]
    size, half = cap + HEADER, n // 2
    strip = (fields * lons * 2, LANES)
    shapes = [(size, LANES), (half * size + strip[0], LANES)]
    shapes += [
        (size if s == half // 2 else 2 * size, LANES) for s in range(1, half)
    ] + [strip]
    hbm = pl.BlockSpec(memory_space=pltpu.HBM)
    vm = pl.BlockSpec(memory_space=V)
    return pl.pallas_call(
        functools.partial(pack_kernel, n, cap, stations),
        out_shape=tuple(V(shape, jnp.float32) for shape in shapes),
        in_specs=[pl.BlockSpec(memory_space=pltpu.SMEM)] + [hbm] * 5,
        out_specs=(vm,) * len(shapes),
        scratch_shapes=[
            V(dep.shape, jnp.float32),
            V((rows, LANES), jnp.int32),
            V((rows, LANES), jnp.int32),
            V((rows, LANES), jnp.int32),
            V((2, fields, lons, 8, LANES), jnp.float32),
            V((n * STRIDE + HEADER + STRIDE, LANES), jnp.float32),
            V((rows, LANES), jnp.int32),
            pltpu.SMEM((rows, LANES), jnp.int32),
            pltpu.SemaphoreType.DMA((6,)),
        ],
        compiler_params=params(),
        name="pack",
    )(count, *(in_hbm(array) for array in (band, station, var, dep, coef)))


def relay_kernel(shifts, size, swapped, *rest):
    for s, to in zip(shifts, rest[len(rest) - len(shifts) :]):
        to[pl.ds(size, size), :] = swapped[pl.ds(s * size, size), :]


def relay(swapped, through, shifts, size, after=()):
    k = len(shifts)
    vm = pl.BlockSpec(memory_space=V)
    picked = [through[s - 1] for s in shifts]
    return pl.pallas_call(
        functools.partial(relay_kernel, shifts, size),
        out_shape=tuple(V(array.shape, jnp.float32) for array in picked),
        in_specs=[vm] * (k + 1 + len(after)),
        out_specs=(vm,) * k,
        input_output_aliases={j + 1: j for j in range(k)},
        compiler_params=params(),
        name="relay",
    )(in_vmem(swapped), *(in_vmem(array) for array in (*picked, *after)))


def alone_kernel(start, swapped, *rest):
    to = rest[-1]
    to[...] = swapped[pl.ds(start, to.shape[0]), :]


def alone(swapped, s, size, after=()):
    vm = pl.BlockSpec(memory_space=V)
    return pl.pallas_call(
        functools.partial(alone_kernel, s * size),
        out_shape=V((size, LANES), jnp.float32),
        in_specs=[vm] * (1 + len(after)),
        out_specs=vm,
        compiler_params=params(),
        name="alone",
    )(in_vmem(swapped), *(in_vmem(array) for array in after))


def open_header(packet, base, cap, view, header, sem):
    view[...] = packet[pl.ds(base + cap, HEADER), :].astype(jnp.int32)
    copy = pltpu.make_async_copy(view, header, sem)
    copy.start()
    return copy


def scatter_packet(table_ref, packet, start, header, state):
    unroll = 8
    count = header[HEADER - 1, 0]

    def some(g, carry):
        base = g * unroll
        major, minor = base >> 7, base & 127
        rows = [table_ref[0, header[major, minor + k]] for k in range(unroll)]
        for k in range(unroll):
            state[pl.ds(rows[k], 1), :] += packet[pl.ds(start + base + k, 1), :]
        return carry

    def one(j, carry):
        row = table_ref[0, header[j >> 7, j & 127]]
        state[pl.ds(row, 1), :] += packet[pl.ds(start + j, 1), :]
        return carry

    whole = count >> 3
    lax.fori_loop(0, whole, some, 0)
    lax.fori_loop(whole * unroll, count, one, 0)


def first_kernel(
    k, lons, lats, cap, table_ref, adjoint_ref, *rest
):
    packets, (state, full) = rest[:k], rest[len(rest) - 2 * k - 3 : len(rest) - 2 * k - 1]
    rest = rest[len(rest) - 2 * k - 1 :]
    views, headers, sem = rest[:k], rest[k : 2 * k], rest[2 * k]
    span = lats + 4
    ring = (lons + 4) * span
    nv = state.shape[0] // ring
    load = pltpu.make_async_copy(adjoint_ref, full, sem.at[0])
    load.start()
    opened = [
        open_header(packets[j], 0, cap, views[j], headers[j], sem.at[j + 1]) for j in range(k)
    ]
    load.wait()

    def fill(i, carry):
        for v in range(nv):
            to = v * ring + (i + 2) * span + 2
            at = (v * lons + i) * lats
            for r in range(0, lats, 8):
                state[pl.ds(to + r, 8), :] = full[pl.ds(pl.multiple_of(at + r, 8), 8), :]
        return carry

    lax.fori_loop(0, lons, fill, 0)
    wait_all(opened)
    for j in range(k):
        scatter_packet(table_ref, packets[j], 0, headers[j], state)


def scatter_first(table, adjoint, packets, cap, shape, after=()):
    nv, lons, lats = shape
    k = len(packets)
    hbm = pl.BlockSpec(memory_space=pltpu.HBM)
    ring = (lons + 4) * (lats + 4)
    return pl.pallas_call(
        functools.partial(first_kernel, k, lons, lats, cap),
        out_shape=V((nv * ring, LANES), jnp.float32),
        in_specs=[pl.BlockSpec(memory_space=pltpu.SMEM), hbm]
        + [pl.BlockSpec(memory_space=V)] * (k + len(after)),
        out_specs=pl.BlockSpec(memory_space=V),
        scratch_shapes=[
            V(adjoint.shape, jnp.float32),
            *[V((HEADER, LANES), jnp.int32)] * k,
            *[pltpu.SMEM((HEADER, LANES), jnp.int32)] * k,
            pltpu.SemaphoreType.DMA((k + 1,)),
        ],
        compiler_params=params(),
        name="scatter_own",
    )(table, in_hbm(adjoint), *(in_vmem(array) for array in (*packets, *after)))


def more_kernel(k, lons, lats, cap, last, table_ref, *rest):
    size = cap + HEADER
    packets = [(rest[j], base) for j in range(k) for base in range(0, rest[j].shape[0], size)]
    m = len(packets)
    rest = rest[len(rest) - (3 if last else 1) - 2 * m - 1 :]
    outs, rest = rest[: 3 if last else 1], rest[3 if last else 1 :]
    views, headers, sem = rest[:m], rest[m : 2 * m], rest[2 * m]
    state = outs[0]
    opened = [
        open_header(*packets[j], cap, views[j], headers[j], sem.at[j]) for j in range(m)
    ]
    wait_all(opened)
    for j in range(m):
        scatter_packet(table_ref, *packets[j], headers[j], state)
    if not last:
        return
    near, across = outs[1:]
    span = lats + 4
    ring = (lons + 4) * span
    nv = state.shape[0] // ring
    near_row, across_row = near_side(2, lats)

    def strip(i, carry):
        for v in range(nv):
            at = v * ring + (i + 2) * span
            to = (v * lons + i) * 2
            near[pl.ds(to, 2), :] = state[pl.ds(at + near_row, 2), :]
            across[pl.ds(to, 2), :] = state[pl.ds(at + across_row, 2), :]
        return carry

    lax.fori_loop(0, lons, strip, 0)


def scatter_more(table, state, packets, cap, shape, last, after=()):
    nv, lons, lats = shape
    k = len(packets)
    m = sum(packet.shape[0] // (cap + HEADER) for packet in packets)
    vm = pl.BlockSpec(memory_space=V)
    out = V(state.shape, jnp.float32)
    strip = V((nv * lons * 2, LANES), jnp.float32)
    return pl.pallas_call(
        functools.partial(more_kernel, k, lons, lats, cap, last),
        out_shape=(out, strip, strip) if last else out,
        in_specs=[pl.BlockSpec(memory_space=pltpu.SMEM)] + [vm] * (k + 1 + len(after)),
        out_specs=(vm, vm, vm) if last else vm,
        input_output_aliases={k + 1: 0},
        scratch_shapes=[V((HEADER, LANES), jnp.int32)] * m
        + [pltpu.SMEM((HEADER, LANES), jnp.int32)] * m
        + [pltpu.SemaphoreType.DMA((m,))],
        compiler_params=params(),
        name="scatter_last" if last else "scatter_more",
    )(
        table,
        *(in_vmem(packet) for packet in packets),
        in_vmem(state),
        *(in_vmem(array) for array in after),
    )


def widen_kernel(coef_ref, swapped_ref, across_ref, ring_out, near_lon, across_lon, own, sem):
    fields, lons, lats, _ = coef_ref.shape
    span = lats + 4
    ring = (lons + 4) * span
    near_from = swapped_ref.shape[0] - fields * lons * 2
    near_row, across_row = near_side(0, lats + 2)
    near_at, across_at = near_side(2 * span, lons * span, "lon")
    run([pltpu.make_async_copy(coef_ref, own, sem)])

    def fill(i, carry):
        for f in range(fields):
            to = f * ring + (i + 2) * span
            at = (f * lons + i) * 2
            for r in range(0, lats, 8):
                ring_out[pl.ds(to + 2 + r, 8), :] = own[f, i, r : r + 8]
            ring_out[pl.ds(to + near_row, 2), :] = swapped_ref[pl.ds(near_from + at, 2), :]
            ring_out[pl.ds(to + across_row, 2), :] = across_ref[pl.ds(at, 2), :]
        return carry

    lax.fori_loop(0, lons, fill, 0)
    take_lons(ring_out, near_lon, across_lon, fields, ring, 2 * span, near_at, across_at)


def take_lons(ring_ref, near, across, count, ring, size, near_at, across_at):
    for f in range(count):
        near[pl.ds(f * size, size), :] = ring_ref[pl.ds(f * ring + near_at, size), :]
        across[pl.ds(f * size, size), :] = ring_ref[pl.ds(f * ring + across_at, size), :]


def put_lons(ring_ref, near, across, count, ring, size, near_at, across_at):
    for f in range(count):
        ring_ref[pl.ds(f * ring + near_at, size), :] = near[pl.ds(f * size, size), :]
        ring_ref[pl.ds(f * ring + across_at, size), :] = across[pl.ds(f * size, size), :]


def widen(coef, swapped, across):
    fields, lons, lats, _ = coef.shape
    span = lats + 4
    vm = pl.BlockSpec(memory_space=V)
    edge = V((fields * 2 * span, LANES), jnp.float32)
    return pl.pallas_call(
        widen_kernel,
        out_shape=(V((fields * (lons + 4) * span, LANES), jnp.float32), edge, edge),
        in_specs=[pl.BlockSpec(memory_space=pltpu.HBM), vm, vm],
        out_specs=(vm, vm, vm),
        scratch_shapes=[V(coef.shape, jnp.float32), pltpu.SemaphoreType.DMA],
        compiler_params=params(),
        name="widen",
    )(in_hbm(coef), in_vmem(swapped), in_vmem(across))


def combine_kernel(lons, lats, ring_ref, near, across, out_ref, field):
    me = lax.axis_index("lat")
    total = lats * lax.axis_size("lat")
    span, rim = lats + 4, lats + 2
    ring = (lons + 4) * span
    size = rim_rows(lons, lats)
    field[...] = ring_ref[...]
    ends = near_side(0, (lons + 2) * span, "lon")
    put_lons(field, near, across, field.shape[0] // ring, ring, 2 * span, *ends)
    lev = lax.broadcasted_iota(jnp.int32, (8, LANES), 1)
    row = lax.broadcasted_iota(jnp.int32, (8, LANES), 0)

    def one(i, carry):
        for r in chunks(rim):
            lat = row + (r - 1) + me * lats
            inside = (lat >= 0) & (lat < total)
            at = (i + 1) * span + r + 1

            def wind(f, shift, at=at):
                return ADVECT_SCALE * field[pl.ds(f * ring + at + shift, 8), :]

            def half(shift, at=at):
                return 0.5 * field[pl.ds(2 * ring + at + shift, 8), :]

            mine = half(0)
            east_factor = wind(0, 0) + (mine + half(span))
            west_factor = (mine + half(-span)) - wind(0, -span)
            north_factor = wind(1, 0) + (mine + half(1))
            south_factor = (mine + half(-1)) - wind(1, -1)
            up = jnp.where(lev < LANES - 1, mine + pltpu.roll(mine, LANES - 1, 1), 0.0)
            down = jnp.where(lev > 0, mine + pltpu.roll(mine, 1, 1), 0.0)
            centre = 1.0 - (
                ((east_factor + west_factor) + (north_factor + south_factor)) + (up + down)
            )
            factors = (centre, east_factor, west_factor, north_factor, south_factor, up, down)
            for k, value in enumerate(factors):
                out_ref[pl.ds(k * size + i * rim + r, 8), :] = jnp.where(inside, value, 0.0)
        return carry

    lax.fori_loop(0, lons + 2, one, 0)


def combine(ring, near, across, lons, lats):
    vm = pl.BlockSpec(memory_space=V)
    return pl.pallas_call(
        functools.partial(combine_kernel, lons, lats),
        out_shape=V((7 * rim_rows(lons, lats), LANES), jnp.float32),
        in_specs=[vm, vm, vm],
        out_specs=vm,
        scratch_shapes=[V(ring.shape, jnp.float32)],
        compiler_params=params(),
        name="combine",
    )(in_vmem(ring), in_vmem(near), in_vmem(across))


def rim_rows(lons, lats):
    return -(-(lons + 2) * (lats + 2) // 8) * 8


def chunks(rows):
    starts = list(range(0, rows - 7, 8))
    if starts[-1] + 8 < rows:
        starts.append(rows - 8)
    return starts


def shift_matrix():
    k = lax.broadcasted_iota(jnp.int32, (2 * LANES, 2 * LANES), 0) & (LANES - 1)
    j = lax.broadcasted_iota(jnp.int32, (2 * LANES, 2 * LANES), 1)
    take = ((j < LANES) & (k == j + 1)) | ((j >= LANES) & (k == j - LANES - 1))
    return take.astype(jnp.float32).astype(jnp.bfloat16)


def shifted(centres, matrix):
    block = jnp.concatenate(centres, axis=0)
    high = block.astype(jnp.bfloat16)
    low = (block - high.astype(jnp.float32)).astype(jnp.bfloat16)
    both = jnp.dot(
        jnp.concatenate([high, low], axis=1), matrix, preferred_element_type=jnp.float32
    )
    return [
        (both[8 * k : 8 * k + 8, :LANES], both[8 * k : 8 * k + 8, LANES:])
        for k in range(len(centres))
    ]


def rolled(centre):
    return pltpu.roll(centre, LANES - 1, 1), pltpu.roll(centre, 1, 1)


def weighted(factors, source, at, east, rows=None, levels=None):
    rows = rows or (lambda start: pl.ds(start, 8))
    centre = source[rows(at), :]
    above, below = levels or rolled(centre)
    total = factors[0] * centre + factors[1] * source[rows(at + east), :]
    other = factors[2] * source[rows(at - east), :] + factors[3] * source[rows(at + 1), :]
    third = factors[4] * source[rows(at - 1), :] + factors[5] * above
    return (total + other) + (third + factors[6] * below)


def step_rows(coef_ref, source, nv, spots, stride, east, put, matrix):
    size = coef_ref.shape[0] // 7
    levels = [None] * (len(spots) * nv)
    if matrix is not None:
        part = int(len(levels) * 0.5) // 2 * 2
        levels[:part] = shifted(
            [source[pl.ds(v * stride + at, 8), :] for _, at in spots for v in range(nv)][:part],
            matrix,
        )
    for k, (row, at) in enumerate(spots):
        factors = [coef_ref[pl.ds(f * size + row, 8), :] for f in range(7)]
        for v in range(nv):
            put(
                k,
                v,
                weighted(
                    factors, source, v * stride + at, east, levels=levels[k * nv + v]
                ),
            )


def first_step(coef_ref, state, mid, nv, lons, lats, places, starts, matrix=None):
    span, rim = lats + 4, lats + 2
    ring, size = (lons + 4) * span, rim_rows(lons, lats)
    spots = [(i * rim + r, (i + 1) * span + r + 1) for i in places for r in starts]

    def put(k, v, value):
        mid[pl.ds(v * size + spots[k][0], 8), :] = value

    step_rows(coef_ref, state, nv, spots, ring, span, put, matrix)


def first_step_along(coef_ref, state, mid, nv, lons, lats, i, r):
    span, rim = lats + 4, lats + 2
    ring, size = (lons + 4) * span, rim_rows(lons, lats)

    def rim_at(start):
        return pl.ds(start, 8, stride=rim)

    def ring_at(start):
        return pl.ds(start, 8, stride=span)

    factors = [coef_ref[rim_at(k * size + i * rim + r), :] for k in range(7)]
    for v in range(nv):
        mid[rim_at(v * size + i * rim + r), :] = weighted(
            factors, state, v * ring + (i + 1) * span + r + 1, span, ring_at
        )


def second_step(coef_ref, mid, out, nv, lons, lats, places, place, matrix=None):
    rim = lats + 2
    spots = [
        ((i + 1) * rim + r + 1, (i + 1) * rim + r + 1) for i in places for r in range(0, lats, 8)
    ]
    each = lats // 8

    def put(k, v, value):
        at = place(v, k // each) + (k % each) * 8
        out[pl.ds(pl.multiple_of(at, 8), 8), :] = value

    step_rows(coef_ref, mid, nv, spots, rim_rows(lons, lats), rim, put, matrix)


def insert_kernel(lons, lats, state_in, near, across, state, near_lon, across_lon):
    span = lats + 4
    ring = (lons + 4) * span
    nv = state.shape[0] // ring

    near_row, across_row = near_side(0, lats + 2)

    def strip(i, carry):
        for v in range(nv):
            at = v * ring + (i + 2) * span
            frm = (v * lons + i) * 2
            state[pl.ds(at + near_row, 2), :] = near[pl.ds(frm, 2), :]
            state[pl.ds(at + across_row, 2), :] = across[pl.ds(frm, 2), :]
        return carry

    lax.fori_loop(0, lons, strip, 0)
    ends = near_side(2 * span, lons * span, "lon")
    take_lons(state, near_lon, across_lon, nv, ring, 2 * span, *ends)


def insert(state, near, across, shape):
    nv, lons, lats = shape
    vm = pl.BlockSpec(memory_space=V)
    edge = V((nv * 2 * (lats + 4), LANES), jnp.float32)
    return pl.pallas_call(
        functools.partial(insert_kernel, lons, lats),
        out_shape=(V(state.shape, jnp.float32), edge, edge),
        in_specs=[vm] * 3,
        out_specs=(vm,) * 3,
        input_output_aliases={0: 0},
        compiler_params=params(),
        name="insert",
    )(in_vmem(state), in_vmem(near), in_vmem(across))


def early_kernel(nv, lons, lats, coef_ref, state, mid):
    starts = [r + 2 for r in chunks(lats - 2)]
    matrix = shift_matrix()

    def first(i, carry):
        at = jnp.minimum(2 + GROUP * i, lons - GROUP)
        places = [at + k for k in range(GROUP)]
        first_step(coef_ref, state, mid, nv, lons, lats, places, starts, matrix)
        return carry

    lax.fori_loop(0, -(-(lons - 2) // GROUP), first, 0)


def early(coef, state, shape):
    nv, lons, lats = shape
    vm = pl.BlockSpec(memory_space=V)
    return pl.pallas_call(
        functools.partial(early_kernel, nv, lons, lats),
        out_shape=V((nv * rim_rows(lons, lats), LANES), jnp.float32),
        in_specs=[vm, vm],
        out_specs=vm,
        compiler_params=params(),
        name="early",
    )(in_vmem(coef), in_vmem(state))


def inner_kernel(lons, lats, coef_ref, state, mid_in, mid, out_ref, out, sem):
    nv = out.shape[0] // (lons * lats)
    cells = lons * lats
    for r in (0, 1, lats, lats + 1):

        def first(k, carry, r=r):
            i = jnp.minimum(2 + 8 * k, lons - 8)
            first_step_along(coef_ref, state, mid, nv, lons, lats, i, r)
            return carry

        lax.fori_loop(0, -(-(lons - 2) // 8), first, 0)

    matrix = shift_matrix()

    def second(i, carry):
        second_step(
            coef_ref,
            mid,
            out,
            nv,
            lons,
            lats,
            [2 + GROUP * i + k for k in range(GROUP)],
            lambda v, k: v * cells + (2 + GROUP * i + k) * lats,
            matrix,
        )
        return carry

    parts = 4
    groups = (lons - 4) // GROUP
    ends = [0] + [groups * p // parts for p in range(1, parts)] + [groups]
    edges = [2 + GROUP * g for g in ends]
    copies = []
    for p in range(parts):
        lax.fori_loop(ends[p], ends[p + 1], second, 0)
        for v in range(nv):
            span = pl.ds(v * cells + edges[p] * lats, (edges[p + 1] - edges[p]) * lats)
            copy = pltpu.make_async_copy(out.at[span], out_ref.at[span], sem.at[p * nv + v])
            copy.start()
            copies.append(copy)
    wait_all(copies)


def inner(coef, state, mid, shape):
    nv, lons, lats = shape
    vm = pl.BlockSpec(memory_space=V)
    return pl.pallas_call(
        functools.partial(inner_kernel, lons, lats),
        out_shape=(
            V(mid.shape, jnp.float32),
            jax.ShapeDtypeStruct((nv * lons * lats, LANES), jnp.float32),
        ),
        in_specs=[vm, vm, vm],
        out_specs=(vm, pl.BlockSpec(memory_space=pltpu.HBM)),
        input_output_aliases={2: 0},
        scratch_shapes=[
            V((nv * lons * lats, LANES), jnp.float32),
            pltpu.SemaphoreType.DMA((4 * nv,)),
        ],
        compiler_params=params(),
        name="inner",
    )(in_vmem(coef), in_vmem(state), in_vmem(mid))


def outer_kernel(
    lons, lats, coef_ref, state_in, mid_in, near, across, out_in, state, mid, out_ref, out, sem
):
    span = lats + 4
    ring = (lons + 4) * span
    nv = state.shape[0] // ring
    cells = lons * lats
    ends = near_side(0, (lons + 2) * span, "lon")
    put_lons(state, near, across, nv, ring, 2 * span, *ends)

    def first(k, carry):
        i = jnp.where(k < 2, k, lons - 2 + k)
        first_step(coef_ref, state, mid, nv, lons, lats, (i,), chunks(lats + 2))
        return carry

    lax.fori_loop(0, 4, first, 0)

    def second(k, carry):
        i = jnp.where(k < 2, k, lons - 4 + k)
        second_step(
            coef_ref, mid, out, nv, lons, lats, (i,), lambda v, _: (v * 4 + k) * lats
        )
        return carry

    lax.fori_loop(0, 4, second, 0)
    copies = []
    for v in range(nv):
        for side, at in ((0, 0), (1, lons - 2)):
            copies.append(
                pltpu.make_async_copy(
                    out.at[pl.ds((v * 4 + 2 * side) * lats, 2 * lats)],
                    out_ref.at[pl.ds(v * cells + at * lats, 2 * lats)],
                    sem.at[v * 2 + side],
                )
            )
    run(copies)


def outer(coef, state, mid, near, across, out, shape):
    nv, lons, lats = shape
    vm = pl.BlockSpec(memory_space=V)
    hbm = pl.BlockSpec(memory_space=pltpu.HBM)
    return pl.pallas_call(
        functools.partial(outer_kernel, lons, lats),
        out_shape=(
            V(state.shape, jnp.float32),
            V(mid.shape, jnp.float32),
            jax.ShapeDtypeStruct(out.shape, jnp.float32),
        ),
        in_specs=[vm] * 5 + [hbm],
        out_specs=(vm, vm, hbm),
        input_output_aliases={1: 0, 2: 1, 5: 2},
        scratch_shapes=[V((nv * 4 * lats, LANES), jnp.float32), pltpu.SemaphoreType.DMA((2 * nv,))],
        compiler_params=params(),
        name="outer",
    )(in_vmem(coef), in_vmem(state), in_vmem(mid), in_vmem(near), in_vmem(across), out)[2]


def body(
    adjoint_in, departures, obs_band, obs_station, obs_var, counts, station_cell, coefficients
):
    nv, lons, lats, levels = adjoint_in.shape
    shape = (nv, lons, lats)
    slots = departures.shape[2]
    n = lax.axis_size("lat")
    cap = -(-3 * slots // n // 8) * 8
    stations = station_cell.shape[2]
    square = (slots // LANES, LANES)
    own, swap, *rest = pack(
        n,
        cap,
        stations,
        counts,
        obs_band.reshape(square),
        obs_station.reshape(square),
        obs_var.reshape(square),
        departures.reshape(slots, levels),
        coefficients,
    )
    through, across = rest[:-1], rest[-1]
    swapped = lax.ppermute(swap, "lat", [(i, i ^ 1) for i in range(n)])
    across = lax.ppermute(across, "lat", pairs_of("lat", False)[1])
    size = cap + HEADER
    order = sorted(range(1, n // 2), key=lambda s: abs(4 * s - n))
    cell = station_cell.reshape(1, stations)
    span = lats + 4
    spot = (cell // lats + 2) * span + cell % lats + 2
    tile = (lons + 4) * span
    table = jnp.concatenate([spot + v * tile for v in range(nv)], axis=1)
    def send(s, packet):
        return lax.ppermute(packet, "lat", [(i, (i + 2 * s) % n) for i in range(n)])

    def send_pairs(shifts, after):
        return [
            send(s, packet)
            for s, packet in zip(shifts, relay(swapped, through, shifts, size, after))
        ]

    middle = 1 + (len(order) - 1) // 2
    adjoint = adjoint_in.reshape(nv * lons * lats, levels)
    ahead = send(order[0], through[order[0] - 1])
    second = send_pairs(order[1:middle], ())
    ring, near, across = widen(coefficients, swapped, across)
    third = send_pairs(order[middle:], (ring,))
    near, across = swap_sides(near, across, "lon", True)
    coef = combine(ring, near, across, lons, lats)
    state = scatter_first(table, adjoint, [own, swapped, ahead], cap, shape, (coef,))
    moved = [send(order[0], alone(swapped, order[0], size, (state,)))]
    state = scatter_more(table, state, second, cap, shape, False)
    state = scatter_more(table, state, third, cap, shape, False)
    state, near, across = scatter_more(table, state, moved, cap, shape, True)
    near, across = swap_sides(near, across, "lat", False)
    mid = early(coef, state, shape)
    state, near, across = insert(state, near, across, shape)
    near, across = swap_sides(near, across, "lon", True)
    mid, out = inner(coef, state, mid, shape)
    out = outer(coef, state, mid, near, across, out, shape)
    return out.reshape(adjoint_in.shape)


def solution(mesh):
    in_specs = (
        P(None, "lon", "lat", None),
        P("lon", "lat", None, None),
        P("lon", "lat", None, None),
        P("lon", "lat", None),
        P("lon", "lat", None),
        P("lon", "lat"),
        P("lon", "lat", None),
        P(None, "lon", "lat", None),
    )
    out_specs = P(None, "lon", "lat", None)
    return jax.shard_map(body, mesh=mesh, in_specs=in_specs, out_specs=out_specs, check_vma=False)
```
